32 devices in a mesh: groups: 2 (over y), space: 4 (over x, core), chan: 4 (over z).
Axes of the slice: x: 2, y: 2, z: 4, core: 2. Of those that a mesh axis runs over, the one named last changes fastest.
Arguments:
- volume: bfloat16 [32, 16, 256, 256], P(('groups', 'space'), 'chan'), parts along dimension 0, may hold values from -6 to 6
- weight: bfloat16 [8, 256, 256], P(None, 'space', 'chan'), may hold values from -0.125 to 0.125
- cotangent: bfloat16 [16, 8, 128, 256], P(('groups', 'space'), None, None, 'chan'), parts along dimension 0, may hold values from -6 to 6
Outputs:
- grad_volume: bfloat16 [32, 16, 256, 256], P(('groups', 'space'), 'chan'), parts along dimension 0
- grad_weight: float32 [16, 256, 256], P('groups', 'space', 'chan'), parts along dimension 0
The draws below stay inside these ranges and needn't reach their ends.
There are 2 independent parts, one for each index of `groups`. The reference program is written for one: setup_inputs(seed, part) draws one part's arguments, and reference() takes and returns one part's arrays. A program takes and returns all parts, laid end to end along the dimension named above; an argument that names none is the same for every part. Nothing has to cross between parts.
All inputs are finite; a program needn't handle non-finite values.
Results may differ from the reference program's by a relative error of at most 0.0049.
Values may be sent and summed in bfloat16 or wider, within the bound.
No kernel may reach another device: no remote copies, remote signals or barrier semaphores. Data moves between devices by JAX's collectives and lax.ppermute only.
A program may use at most 64 MiB of HBM per device.

```python
import jax
import jax.numpy as jnp
from jax import lax

CIN = 256
COUT = 256
NZ = 256
NX = 16
NY = 16
TILE_OUT = 512


def with_spikes(drawn, key, source, target, blocks, factor):
    def block_of(position):
        return (jnp.arange(drawn.shape[position]) // (drawn.shape[position] // blocks)).reshape((-1,) + (1,) * (drawn.ndim - 1 - position))

    one_side = jax.random.permutation(key, blocks)[block_of(target)]
    other_side = (block_of(target) + blocks // 2) % blocks
    return jnp.where((block_of(source) == one_side) | (block_of(source) == other_side), factor * drawn, drawn)


def steps_of(stream_key, extent, shards, low, high):
    factor_of, own = 1.0, jax.random.fold_in(stream_key, 6)
    for axis_at, blocks in shards:
        heights = jnp.exp(jax.random.uniform(jax.random.fold_in(own, axis_at), (blocks,), jnp.float32, low / len(shards), high / len(shards)))
        factor_of = factor_of * jnp.repeat(heights, extent[axis_at] // blocks).reshape([-1 if axis == axis_at else 1 for axis in range(len(extent))])
    return factor_of


def normal_values(key, extent, width, most, pieces=(), dtype=jnp.bfloat16):
    loudness = steps_of(key, extent, pieces, -0.22, 0.18) if pieces else 1.0
    result = jax.random.normal(key, extent, jnp.float32) * width * loudness
    return jnp.minimum(jnp.maximum(result, -most), most).astype(dtype)


def noise_with(key, dims, deviation, limit, split, heavy, kind=jnp.bfloat16):
    values = deviation * jax.random.normal(key, dims, jnp.float32)
    if split:
        values = values * steps_of(key, dims, split, -0.22, 0.18)
    return jnp.clip(with_spikes(values, jax.random.fold_in(key, 3), *heavy), -limit, limit).astype(kind)


def setup_inputs(seed: int = 0, part: int = 0) -> dict:
    key_list = jax.random.split(jax.random.key(seed), 4)
    own_keys = jax.random.split(jax.random.fold_in(key_list[3], part), 4)
    volume = noise_with(own_keys[0], (NX, NY, NZ, CIN), 1.0, 6.0, ((0, 4), (1, 4)), (0, 3, 4, 2.0))
    weight = normal_values(key_list[1], (8, CIN, COUT), (8 * CIN) ** -0.5, 0.125, ((1, 4), (2, 4)))
    cotangent = noise_with(own_keys[2], (NX // 2, NY // 2, NZ // 2, COUT), 1.0, 6.0, ((0, 4), (3, 4)), (1, 3, 4, 2.0))
    return {"volume": volume, "weight": weight, "cotangent": cotangent}


def reference(volume, weight, cotangent):
    in_chan = volume.shape[3]
    out_chan = weight.shape[2]
    planes = volume.shape[0] // 2
    w_matrix = weight.reshape(8 * in_chan, out_chan)
    slab_pairs = volume.reshape(planes, 2, NY, NZ, in_chan)

    def advance(summed, inputs_pair):
        slab_rows, upstream = inputs_pair
        patches = slab_rows.reshape(2, NY // 2, 2, NZ // 2, 2, in_chan)
        patches = patches.transpose(1, 3, 0, 2, 4, 5).reshape(-1, 8 * in_chan)
        pre_act = jnp.dot(patches, w_matrix, preferred_element_type=jnp.float32)
        squash = jax.nn.sigmoid(pre_act)
        slopes = squash * (1.0 + pre_act * (1.0 - squash))
        deltas = (upstream.reshape(-1, out_chan).astype(jnp.float32) * slopes).astype(jnp.bfloat16)
        summed = summed + jnp.dot(patches.T, deltas, preferred_element_type=jnp.float32)
        grad_rows = jnp.dot(deltas, w_matrix.T, preferred_element_type=jnp.float32).astype(jnp.bfloat16)
        grad_slab = grad_rows.reshape(NY // 2, NZ // 2, 2, 2, 2, in_chan)
        grad_slab = grad_slab.transpose(2, 0, 3, 1, 4, 5).reshape(2, NY, NZ, in_chan)
        return summed, grad_slab

    initial = jnp.zeros((8 * in_chan, out_chan), jnp.float32)
    summed, grad_slabs = lax.scan(advance, initial, (slab_pairs, cotangent))
    grad_volume = grad_slabs.reshape(volume.shape)
    grad_weight = (summed / TILE_OUT).reshape(8, in_chan, out_chan)
    return (grad_volume, grad_weight)
```

```python
import functools

import jax
import jax.numpy as jnp
from jax import lax
from jax.experimental import pallas as pl
from jax.experimental.pallas import tpu as pltpu
from jax.sharding import PartitionSpec as P

LANES = 128
BF16 = jnp.bfloat16
F32 = jnp.float32


def other(me, step):
    return me ^ step


def fetch(x, axis, pairs):
    return lax.ppermute(x, axis, pairs)


def lane_group(shape, width):
    return lax.broadcasted_iota(jnp.int32, shape, len(shape) - 1) // width


def merge(parts, width, flip):
    group = lane_group(parts[0].shape, width)
    out = parts[flip]
    for g in range(1, len(parts)):
        out = jnp.where(group == g, parts[g ^ flip], out)
    return out


def swap_groups(x, width, flip):
    if flip == 0:
        return x
    tiles = []
    for t in range(x.shape[1] // LANES):
        tile = x[:, t * LANES:(t + 1) * LANES]
        bit = 1
        while bit <= flip:
            if flip & bit:
                shift = width * bit
                up = pltpu.roll(tile, LANES - shift, 1)
                if 2 * shift == LANES:
                    tile = up
                else:
                    even = (lane_group(tile.shape, shift) % 2) == 0
                    tile = jnp.where(even, up, pltpu.roll(tile, shift, 1))
            bit *= 2
        tiles.append(tile)
    return tiles[0] if len(tiles) == 1 else jnp.concatenate(tiles, axis=1)


def whole(x):
    return pl.BlockSpec(x.shape, lambda *_: (0,) * len(x.shape))


def params():
    return pltpu.CompilerParams(vmem_limit_bytes=48 * 1024 * 1024)


def cost(flops, bytes_accessed):
    return pl.CostEstimate(flops=flops, bytes_accessed=bytes_accessed, transcendentals=0)


def spread(x, width, at):
    if width >= LANES:
        return x
    zeros = jnp.zeros((x.shape[0], LANES - width), x.dtype)
    full = jnp.concatenate([x, zeros], axis=1)
    return pltpu.roll(full, at * width, 1) if at else full


def pack_weight(weight, ratio):
    kinds, rows, width = weight.shape
    groups = kinds // ratio
    lanes = ratio * width

    def body(w_ref, *outs):
        for g in range(groups):
            for flip in range(ratio):
                acc = None
                for lane in range(ratio):
                    part = spread(w_ref[g * ratio + (lane ^ flip)].astype(F32), width, lane)
                    acc = part if acc is None else acc + part
                outs[flip][g] = acc.astype(BF16)

    return pl.pallas_call(
        body,
        out_shape=[jax.ShapeDtypeStruct((groups, rows, lanes), BF16)] * ratio,
        compiler_params=params(),
        name="pack_weight",
    )(weight)


def pack_cot(cot, chans, ratio):
    planes, cells_y, cells_z, width = cot.shape
    own_y = cells_y // chans
    cells = planes * own_y * cells_z
    sect = cells // ratio

    def body(c_ref, *outs):
        me = lax.axis_index("chan")
        for step in range(chans):
            flip = step % ratio
            target = other(me, step) * own_y
            mine = []
            for p in range(planes):
                for y in range(own_y):
                    mine.append(c_ref[p, target + y].astype(F32))
            rows = jnp.concatenate(mine, axis=0)
            acc = None
            for lane in range(ratio):
                sec = lane ^ flip
                part = spread(rows[sec * sect:(sec + 1) * sect], width, lane)
                acc = part if acc is None else acc + part
            outs[step][...] = acc.astype(BF16)

    return pl.pallas_call(
        body,
        out_shape=[jax.ShapeDtypeStruct((sect, ratio * width), BF16)] * chans,
        compiler_params=params(),
        name="pack_cot",
    )(cot)


def patch_rows(volume):
    cells_x, cells_y, cells_z, in_chan = volume.shape
    nx, ny, nz = cells_x // 2, cells_y // 2, cells_z // 2

    def body(v_ref, p_ref, t_ref):
        row = lax.broadcasted_iota(jnp.int32, (cells_z, cells_z), 0)
        col = lax.broadcasted_iota(jnp.int32, (cells_z, cells_z), 1)
        pick = (col == 2 * (row % nz) + row // nz).astype(F32).astype(BF16)
        for a in range(2):
            for b in range(2):
                k = 4 * a + 2 * b
                got = jnp.dot(pick, v_ref[a, b], preferred_element_type=F32)
                for e in range(2):
                    part = got[e * nz:(e + 1) * nz]
                    p_ref[k + e] = part.astype(BF16)
                    t_ref[k + e] = part.T.astype(BF16)

    rows = nx * ny * nz
    return pl.pallas_call(
        body,
        grid=(nx * ny,),
        in_specs=[pl.BlockSpec((2, 2, cells_z, in_chan), lambda n: (n // ny, n % ny, 0, 0))],
        out_specs=[
            pl.BlockSpec((8, nz, in_chan), lambda n: (0, n, 0)),
            pl.BlockSpec((8, in_chan, nz), lambda n: (0, 0, n)),
        ],
        out_shape=[
            jax.ShapeDtypeStruct((8, rows, in_chan), BF16),
            jax.ShapeDtypeStruct((8, in_chan, rows), BF16),
        ],
        compiler_params=params(),
        cost_estimate=cost(16 * rows * in_chan * cells_z, 6 * volume.size),
        name="patch_rows",
    )(volume)


def forward(patches, pieces, cots, spaces, chans, ratio):
    kinds, rows, in_chan = patches.shape
    groups, block, lanes = pieces[0][0].shape
    out_chan = lanes * (chans // ratio)
    width = lanes // ratio
    flat = [p for line in pieces for p in line]
    sect = rows // ratio

    def body(p_ref, *refs):
        ins = refs[:len(flat)]
        cot_refs = refs[len(flat):len(flat) + chans]
        d_ref, w_ref = refs[len(flat) + chans:]
        me = lax.axis_index("space")
        for j in range(spaces):
            at = pl.multiple_of(other(me, j) * block, block)
            for g in range(groups):
                for t in range(chans // ratio):
                    got = [ins[j * chans + t * ratio + u][g] for u in range(ratio)]
                    for q in range(ratio):
                        w_ref[g * ratio + q, pl.ds(at, block), t * lanes:(t + 1) * lanes] = merge(got, width, q)
        for sec in range(ratio):
            here = slice(sec * sect, (sec + 1) * sect)
            pre = None
            for q in range(ratio):
                acc = None
                for k in range(q, kinds, ratio):
                    part = jnp.dot(p_ref[k, here], w_ref[k], preferred_element_type=F32)
                    acc = part if acc is None else acc + part
                acc = swap_groups(acc, width, q)
                pre = acc if pre is None else pre + acc
            ups = []
            for t in range(chans // ratio):
                got = [cot_refs[t * ratio + u][...] for u in range(ratio)]
                ups.append(merge(got, width, sec).astype(F32))
            up = swap_groups(jnp.concatenate(ups, axis=1), width, sec)
            squash = 1.0 / (1.0 + jnp.exp(-pre))
            slopes = squash * (1.0 + pre * (1.0 - squash))
            delta = (up * slopes).astype(BF16)
            d_ref[0, here] = delta
            for q in range(1, ratio):
                d_ref[q, here] = swap_groups(delta.astype(F32), width, q).astype(BF16)

    return pl.pallas_call(
        body,
        out_shape=[
            jax.ShapeDtypeStruct((ratio, rows, out_chan), BF16),
            jax.ShapeDtypeStruct((kinds, in_chan, out_chan), BF16),
        ],
        compiler_params=params(),
        cost_estimate=cost(2 * patches.size * out_chan, 2 * patches.size),
        name="forward",
    )(patches, *flat, *cots)


def weight_part(turned, deltas, steps, spaces, dtype):
    kinds, in_chan, rows = turned.shape
    ratio, _, out_chan = deltas.shape
    block = in_chan // spaces

    def body(t_ref, d_ref, *outs):
        me = lax.axis_index("space")
        for n, step in enumerate(steps):
            at = pl.multiple_of(other(me, step) * block, block)
            for k in range(kinds):
                got = jnp.dot(t_ref[k, pl.ds(at, block)], d_ref[k % ratio], preferred_element_type=F32)
                outs[n][k] = got.astype(dtype)

    return pl.pallas_call(
        body,
        out_shape=[jax.ShapeDtypeStruct((kinds, block, out_chan), dtype)] * len(steps),
        compiler_params=params(),
        cost_estimate=cost(2 * turned.size * out_chan * len(steps) // spaces, 2 * turned.size),
        name="weight_part",
    )(turned, deltas)


def add_pairs(mine, theirs, dtypes):
    def body(*refs):
        n = len(mine)
        for i in range(n):
            refs[2 * n + i][...] = (refs[i][...].astype(F32) + refs[n + i][...].astype(F32)).astype(dtypes[i])

    return pl.pallas_call(
        body,
        out_shape=[jax.ShapeDtypeStruct(m.shape, d) for m, d in zip(mine, dtypes)],
        compiler_params=params(),
        name="add_pairs",
    )(*mine, *theirs)


def add_and_pack(mine, theirs, chans, ratio):
    kinds, block, out_chan = mine.shape
    width = out_chan // chans
    lanes = ratio * width
    groups = kinds // ratio

    def body(*refs):
        ins, outs = refs[:1 + len(theirs)], refs[1 + len(theirs):]
        for g in range(groups):
            for t in range(chans // ratio):
                lane = slice(t * lanes, (t + 1) * lanes)
                sums = []
                for q in range(ratio):
                    acc = ins[0][g * ratio + q, :, lane]
                    for ref in ins[1:]:
                        acc = acc + ref[g * ratio + q, :, lane].astype(F32)
                    sums.append(acc)
                for u in range(ratio):
                    packed = swap_groups(merge(sums, width, u), width, u)
                    out = outs[t * ratio + u]
                    out[g] = packed.astype(out.dtype)

    return pl.pallas_call(
        body,
        out_shape=[jax.ShapeDtypeStruct((groups, block, lanes), BF16 if i else F32) for i in range(chans)],
        compiler_params=params(),
        name="add_and_pack",
    )(mine, *theirs)


def finish(parts, kinds, width, scale):
    groups, block, lanes = parts[0].shape
    ratio = lanes // width

    def body(*refs):
        out = refs[-1]
        for g in range(groups):
            acc = refs[0][g]
            for ref in refs[1:-1]:
                acc = acc + ref[g].astype(F32)
            acc = acc * scale
            for q in range(ratio):
                moved = pltpu.roll(acc, lanes - q * width, 1) if q else acc
                out[g * ratio + q] = moved[:, :width]

    return pl.pallas_call(
        body,
        out_shape=jax.ShapeDtypeStruct((kinds, block, width), F32),
        compiler_params=params(),
        name="finish",
    )(*parts)


def volume_grad(deltas, weights, shape):
    cells_x, cells_y, cells_z, in_chan = shape
    nx, ny, nz = cells_x // 2, cells_y // 2, cells_z // 2
    ratio, rows, out_chan = deltas.shape

    def body(d_ref, w_ref, o_ref):
        row = lax.broadcasted_iota(jnp.int32, (cells_z, nz), 0)
        col = lax.broadcasted_iota(jnp.int32, (cells_z, nz), 1)
        wide = {}
        for k in range(8):
            e, q = k % 2, k % ratio
            if (e, q) not in wide:
                put = (row == 2 * col + e).astype(F32).astype(BF16)
                wide[e, q] = jnp.dot(put, d_ref[q], preferred_element_type=F32).astype(BF16)
        for a in range(2):
            for b in range(2):
                acc = None
                for e in range(2):
                    k = 4 * a + 2 * b + e
                    part = lax.dot_general(
                        wide[e, k % ratio], w_ref[k], (((1,), (1,)), ((), ())), preferred_element_type=F32
                    )
                    acc = part if acc is None else acc + part
                o_ref[a, b] = acc.astype(BF16)

    return pl.pallas_call(
        body,
        grid=(nx * ny,),
        in_specs=[pl.BlockSpec((ratio, nz, out_chan), lambda n: (0, n, 0)), whole(weights)],
        out_specs=pl.BlockSpec((2, 2, cells_z, in_chan), lambda n: (n // ny, n % ny, 0, 0)),
        out_shape=jax.ShapeDtypeStruct(shape, BF16),
        compiler_params=params(),
        cost_estimate=cost(32 * rows * in_chan * out_chan, 2 * rows * 8 * in_chan),
        name="volume_grad",
    )(deltas, weights)


def shards(spaces, chans, volume, weight, cotangent):
    kinds, block, width = weight.shape
    ratio = max(1, LANES // width)
    out_rows = volume.shape[0] * volume.shape[1] * volume.shape[2] // 8

    def pairs(count, step):
        return [(d, other(d, step)) for d in range(count)]

    packed = pack_weight(weight, ratio)
    line = [packed[0]] + [
        fetch(packed[i % ratio], "chan", pairs(chans, i)) for i in range(1, chans)
    ]
    cot_out = pack_cot(cotangent, chans, ratio)
    cots = [cot_out[0]] + [
        fetch(cot_out[i], "chan", pairs(chans, i)) for i in range(1, chans)
    ]
    pieces = [line] + [None] * (spaces - 1)
    for j in range(2, spaces, 2):
        pieces[j] = [fetch(p, "space", pairs(spaces, j)) for p in line]
    for j in range(0, spaces, 2):
        pieces[j + 1] = [fetch(p, "space", pairs(spaces, 1)) for p in pieces[j]]
    patches, turned = patch_rows(volume)
    deltas, weights = forward(patches, pieces, cots, spaces, chans, ratio)
    steps = list(range(0, spaces, 2))
    away = weight_part(turned, deltas, [s + 1 for s in steps], spaces, BF16)
    near = weight_part(turned, deltas, steps, spaces, F32)
    crossed = [fetch(p, "space", pairs(spaces, 1)) for p in away]
    sums = add_pairs(near, crossed, [F32] + [BF16] * (len(steps) - 1))
    came = [fetch(sums[n], "space", pairs(spaces, steps[n])) for n in range(1, len(steps))]
    parts = add_and_pack(sums[0], came, chans, ratio)
    got = [parts[0]] + [fetch(parts[i], "chan", pairs(chans, i)) for i in range(1, chans)]
    grad_weight = finish(got, kinds, width, 1.0 / out_rows)
    grad_volume = volume_grad(deltas, weights, volume.shape)
    return (grad_volume, grad_weight)


def solution(mesh):
    return jax.shard_map(
        functools.partial(shards, mesh.shape["space"], mesh.shape["chan"]),
        mesh=mesh,
        in_specs=(
            P(("groups", "space"), "chan", None, None),
            P(None, "space", "chan"),
            P(("groups", "space"), None, None, "chan"),
        ),
        out_specs=(P(("groups", "space"), "chan", None, None), P("groups", "space", "chan")),
        check_vma=False,
    )
```

```python
import functools

import jax
import jax.numpy as jnp
from jax import lax
from jax.experimental import pallas as pl
from jax.experimental.pallas import tpu as pltpu
from jax.sharding import PartitionSpec as P

LANES = 128
TURN_FLOPS = 4 * 10**9
BF16 = jnp.bfloat16
F32 = jnp.float32


def other(me, step):
    return me ^ step


def fetch(x, axis, pairs):
    return lax.ppermute(x, axis, pairs)


def lane_group(shape, width):
    return lax.broadcasted_iota(jnp.int32, shape, len(shape) - 1) // width


def merge(parts, width, flip):
    group = lane_group(parts[0].shape, width)
    out = parts[flip]
    for g in range(1, len(parts)):
        out = jnp.where(group == g, parts[g ^ flip], out)
    return out


def swap_groups(x, width, flip):
    if flip == 0:
        return x
    tiles = []
    for t in range(x.shape[1] // LANES):
        tile = x[:, t * LANES:(t + 1) * LANES]
        bit = 1
        while bit <= flip:
            if flip & bit:
                shift = width * bit
                up = pltpu.roll(tile, LANES - shift, 1)
                if 2 * shift == LANES:
                    tile = up
                else:
                    even = (lane_group(tile.shape, shift) % 2) == 0
                    tile = jnp.where(even, up, pltpu.roll(tile, shift, 1))
            bit *= 2
        tiles.append(tile)
    return tiles[0] if len(tiles) == 1 else jnp.concatenate(tiles, axis=1)


def whole(x):
    return pl.BlockSpec(x.shape, lambda *_: (0,) * len(x.shape))


def params():
    return pltpu.CompilerParams(vmem_limit_bytes=48 * 1024 * 1024)


def cost(flops, bytes_accessed):
    return pl.CostEstimate(flops=flops, bytes_accessed=bytes_accessed, transcendentals=0)


def spread(x, width, at):
    if width >= LANES:
        return x
    zeros = jnp.zeros((x.shape[0], LANES - width), x.dtype)
    full = jnp.concatenate([x, zeros], axis=1)
    return pltpu.roll(full, at * width, 1) if at else full


def pack_weight(weight, ratio):
    kinds, rows, width = weight.shape
    groups = kinds // ratio
    lanes = ratio * width

    def body(w_ref, *outs):
        for g in range(groups):
            for flip in range(ratio):
                acc = None
                for lane in range(ratio):
                    part = spread(w_ref[g * ratio + (lane ^ flip)].astype(F32), width, lane)
                    acc = part if acc is None else acc + part
                outs[flip][g] = acc.astype(BF16)

    return pl.pallas_call(
        body,
        out_shape=[jax.ShapeDtypeStruct((groups, rows, lanes), BF16)] * ratio,
        compiler_params=params(),
        name="pack_weight",
    )(weight)


def pack_cot(cot, chans):
    planes, cells_y, width, cells_z = cot.shape
    own_y = cells_y // chans

    def body(c_ref, *outs):
        me = lax.axis_index("chan")
        for step in range(chans):
            target = other(me, step) * own_y
            for p in range(planes):
                for y in range(own_y):
                    outs[step][p * own_y + y] = c_ref[p, target + y]

    return pl.pallas_call(
        body,
        out_shape=[jax.ShapeDtypeStruct((planes * own_y, width, cells_z), BF16)] * chans,
        compiler_params=params(),
        name="pack_cot",
    )(cot)


def merge_tile(parts, width, after=()):
    groups, block, lanes = parts[0].shape
    ratio = len(parts)

    def body(*refs):
        out = refs[-1]
        for g in range(groups):
            got = [refs[u][g] for u in range(ratio)]
            for q in range(ratio):
                out[g * ratio + q] = merge(got, width, q)

    return pl.pallas_call(
        body,
        in_specs=[pl.BlockSpec(memory_space=pltpu.VMEM)] * ratio + [pl.BlockSpec(memory_space=pl.ANY)] * len(after),
        out_shape=jax.ShapeDtypeStruct((groups * ratio, block, lanes), BF16),
        compiler_params=params(),
        name="merge_tile",
    )(*parts, *after)


def gate(tile, after):
    def body(t_ref, *refs):
        refs[-1][...] = t_ref[...]

    return pl.pallas_call(
        body,
        in_specs=[pl.BlockSpec(memory_space=pltpu.VMEM)] + [pl.BlockSpec(memory_space=pl.ANY)] * len(after),
        out_shape=jax.ShapeDtypeStruct(tile.shape, tile.dtype),
        compiler_params=params(),
        name="gate",
    )(tile, *after)


def patch_rows(volume, after=()):
    cells_x, cells_y, cells_z, in_chan = volume.shape
    nx, ny, nz = cells_x // 2, cells_y // 2, cells_z // 2
    rows = nx * ny * nz

    def body(v_ref, *refs):
        p_ref, t_ref = refs[-2:]
        row = lax.broadcasted_iota(jnp.int32, (cells_z, cells_z), 0)
        col = lax.broadcasted_iota(jnp.int32, (cells_z, cells_z), 1)
        pick = (col == 2 * (row % nz) + row // nz).astype(F32).astype(BF16)
        for n in range(nx * ny):
            here = slice(n * nz, (n + 1) * nz)
            for a in range(2):
                for b in range(2):
                    k = 4 * a + 2 * b
                    got = jnp.dot(pick, v_ref[2 * (n // ny) + a, 2 * (n % ny) + b], preferred_element_type=F32)
                    got = got.astype(BF16)
                    for e in range(2):
                        part = got[e * nz:(e + 1) * nz]
                        p_ref[k + e, here] = part
                        t_ref[k + e, :, here] = part.T

    return pl.pallas_call(
        body,
        in_specs=[pl.BlockSpec(memory_space=pltpu.VMEM)] + [pl.BlockSpec(memory_space=pl.ANY)] * len(after),
        out_shape=[
            jax.ShapeDtypeStruct((8, rows, in_chan), BF16),
            jax.ShapeDtypeStruct((8, in_chan, rows), BF16),
        ],
        compiler_params=params(),
        cost_estimate=cost(16 * rows * in_chan * cells_z, 6 * volume.size),
        name="patch_rows",
    )(volume, *after)


def turn_cot(cots):
    tiles, width, cells = cots[0].shape
    out_chan = width * len(cots)

    def body(*refs):
        out = refs[-1]
        for n in range(tiles):
            column = jnp.concatenate([ref[n] for ref in refs[:-1]], axis=0)
            out[n * cells:(n + 1) * cells] = column.T

    return pl.pallas_call(
        body,
        out_shape=jax.ShapeDtypeStruct((tiles * cells, out_chan), BF16),
        compiler_params=params(),
        cost_estimate=cost(TURN_FLOPS, 4 * tiles * cells * out_chan),
        name="turn_cot",
    )(*cots)


def forward(patches, lines, upstream, width, ratio):
    kinds, rows, in_chan = patches.shape
    _, block, lanes = lines[0][0].shape
    spaces, lane_tiles = len(lines), len(lines[0])
    out_chan = lane_tiles * lanes
    flat = [tile for line in lines for tile in line]

    def body(p_ref, u_ref, *refs):
        ins = refs[:len(flat)]
        d_ref, w_ref = refs[-2:]
        me = lax.axis_index("space")
        for j in range(spaces):
            at = pl.multiple_of(other(me, j) * block, block)
            for t in range(lane_tiles):
                for k in range(kinds):
                    w_ref[k, pl.ds(at, block), t * lanes:(t + 1) * lanes] = ins[j * lane_tiles + t][k]
        part_rows = rows // 2
        for first in range(0, rows, part_rows):
            here = slice(first, first + part_rows)
            pre = None
            for q in range(ratio):
                acc = None
                for k in range(q, kinds, ratio):
                    part = jnp.dot(p_ref[k, here], w_ref[k], preferred_element_type=F32)
                    acc = part if acc is None else acc + part
                acc = swap_groups(acc, width, q)
                pre = acc if pre is None else pre + acc
            up = u_ref[here].astype(F32)
            squash = 1.0 / (1.0 + jnp.exp(-pre))
            slopes = squash * (1.0 + pre * (1.0 - squash))
            delta = (up * slopes).astype(BF16)
            d_ref[0, here] = delta
            for q in range(1, ratio):
                d_ref[q, here] = swap_groups(delta.astype(F32), width, q).astype(BF16)

    return pl.pallas_call(
        body,
        out_shape=[
            jax.ShapeDtypeStruct((ratio, rows, out_chan), BF16),
            jax.ShapeDtypeStruct((kinds, in_chan, out_chan), BF16),
        ],
        compiler_params=params(),
        cost_estimate=cost(2 * patches.size * out_chan, 2 * patches.size),
        name="forward",
    )(patches, upstream, *flat)


def weight_part(turned, deltas, steps, spaces, lanes, dtype):
    kinds, in_chan, rows = turned.shape
    ratio, _, out_chan = deltas.shape
    block = in_chan // spaces
    tiles = out_chan // lanes

    def body(t_ref, d_ref, *outs):
        me = lax.axis_index("space")
        ats = [pl.multiple_of(other(me, step) * block, block) for step in steps]
        for q in range(ratio):
            ks = range(q, kinds, ratio)
            for n, at in enumerate(ats):
                left = jnp.concatenate([t_ref[k, pl.ds(at, block)] for k in ks], axis=0)
                got = jnp.dot(left, d_ref[q], preferred_element_type=F32).astype(dtype)
                for i, k in enumerate(ks):
                    for t in range(tiles):
                        outs[t][n, k] = got[i * block:(i + 1) * block, t * lanes:(t + 1) * lanes]

    return pl.pallas_call(
        body,
        out_shape=[jax.ShapeDtypeStruct((len(steps), kinds, block, lanes), dtype)] * tiles,
        compiler_params=params(),
        cost_estimate=cost(2 * turned.size * out_chan * len(steps) // spaces, 2 * turned.size),
        name="weight_part",
    )(turned, deltas)


def add_core(mine, theirs):
    count, kinds, block, lanes = mine.shape

    def body(a_ref, b_ref, *outs):
        for n in range(count):
            outs[n][...] = (a_ref[n] + b_ref[n].astype(F32)).astype(outs[n].dtype)

    return pl.pallas_call(
        body,
        out_shape=[jax.ShapeDtypeStruct((kinds, block, lanes), BF16 if n else F32) for n in range(count)],
        compiler_params=params(),
        name="add_core",
    )(mine, theirs)


def add_and_pack(mine, theirs, width, own):
    kinds, block, lanes = mine.shape
    ratio = lanes // width
    groups = kinds // ratio

    def body(*refs):
        ins, outs = refs[:1 + len(theirs)], refs[1 + len(theirs):]
        for g in range(groups):
            sums = []
            for q in range(ratio):
                acc = ins[0][g * ratio + q]
                for ref in ins[1:]:
                    acc = acc + ref[g * ratio + q].astype(F32)
                sums.append(acc)
            for u in range(ratio):
                packed = swap_groups(merge(sums, width, u), width, u)
                outs[u][g] = packed.astype(outs[u].dtype)

    return pl.pallas_call(
        body,
        out_shape=[
            jax.ShapeDtypeStruct((groups, block, lanes), F32 if own and u == 0 else BF16) for u in range(ratio)
        ],
        compiler_params=params(),
        name="add_and_pack",
    )(mine, *theirs)


def finish(parts, kinds, width, scale):
    groups, block, lanes = parts[0].shape
    ratio = lanes // width

    def body(*refs):
        out = refs[-1]
        for g in range(groups):
            acc = refs[0][g]
            for ref in refs[1:-1]:
                acc = acc + ref[g].astype(F32)
            acc = acc * scale
            for q in range(ratio):
                moved = pltpu.roll(acc, lanes - q * width, 1) if q else acc
                out[g * ratio + q] = moved[:, :width]

    return pl.pallas_call(
        body,
        out_shape=jax.ShapeDtypeStruct((kinds, block, width), F32),
        compiler_params=params(),
        name="finish",
    )(*parts)


def volume_grad(deltas, weights, shape):
    cells_x, cells_y, cells_z, in_chan = shape
    nx, ny, nz = cells_x // 2, cells_y // 2, cells_z // 2
    ratio, rows, out_chan = deltas.shape

    def body(d_ref, w_ref, o_ref):
        row = lax.broadcasted_iota(jnp.int32, (cells_z, nz), 0)
        col = lax.broadcasted_iota(jnp.int32, (cells_z, nz), 1)
        wide = {}
        for k in range(8):
            e, q = k % 2, k % ratio
            if (e, q) not in wide:
                put = (row == 2 * col + e).astype(F32).astype(BF16)
                wide[e, q] = jnp.dot(put, d_ref[q], preferred_element_type=F32).astype(BF16)
        for a in range(2):
            for b in range(2):
                acc = None
                for e in range(2):
                    k = 4 * a + 2 * b + e
                    part = lax.dot_general(
                        wide[e, k % ratio], w_ref[k], (((1,), (1,)), ((), ())), preferred_element_type=F32
                    )
                    acc = part if acc is None else acc + part
                o_ref[a, b] = acc.astype(BF16)

    return pl.pallas_call(
        body,
        grid=(nx * ny,),
        in_specs=[pl.BlockSpec((ratio, nz, out_chan), lambda n: (0, n, 0)), whole(weights)],
        out_specs=pl.BlockSpec((2, 2, cells_z, in_chan), lambda n: (n // ny, n % ny, 0, 0)),
        out_shape=jax.ShapeDtypeStruct(shape, BF16),
        compiler_params=params(),
        cost_estimate=cost(32 * rows * in_chan * out_chan, 2 * rows * 8 * in_chan),
        name="volume_grad",
    )(deltas, weights)


def shards(spaces, chans, volume, weight, cotangent):
    kinds, block, width = weight.shape
    ratio = max(1, LANES // width)
    out_rows = volume.shape[0] * volume.shape[1] * volume.shape[2] // 8

    def pairs(count, step):
        return [(d, other(d, step)) for d in range(count)]

    packed = pack_weight(weight, ratio)
    tiles = pack_cot(cotangent.transpose(0, 1, 3, 2), chans)
    line = [packed[0]] + [fetch(packed[i % ratio], "chan", pairs(chans, i)) for i in range(1, chans)]
    cots = [tiles[0]] + [fetch(tiles[i], "chan", pairs(chans, i)) for i in range(1, chans)]
    lane_tiles = chans // ratio
    own = [merge_tile(line[t * ratio:(t + 1) * ratio], width) for t in range(lane_tiles)]
    upstream = turn_cot(cots)
    patches, turned = patch_rows(volume, own[1:])
    lines = []
    for j in range(0, spaces, 2):
        lines.append([fetch(tile, "space", pairs(spaces, j)) for tile in own] if j else own)
        lines.append([fetch(gate(tile, (upstream,)) if not j else tile, "space", pairs(spaces, 1)) for t, tile in enumerate(lines[-1])])
    deltas, weights = forward(patches, lines, upstream, width, ratio)
    steps = list(range(0, spaces, 2))
    lanes = ratio * width
    away = weight_part(turned, deltas, [s + 1 for s in steps], spaces, lanes, BF16)
    crossed = [fetch(tile, "space", pairs(spaces, 1)) for tile in away]
    near = weight_part(turned, deltas, steps, spaces, lanes, F32)
    got = [None] * chans
    for t in reversed(range(lane_tiles)):
        sums = add_core(near[t], crossed[t])
        came = [fetch(sums[n], "space", pairs(spaces, steps[n])) for n in range(1, len(steps))]
        parts = add_and_pack(sums[0], came, width, t == 0)
        for u in range(ratio):
            i = t * ratio + u
            got[i] = fetch(parts[u], "chan", pairs(chans, i)) if i else parts[u]
    grad_weight = finish(got, kinds, width, 1.0 / out_rows)
    grad_volume = volume_grad(deltas, weights, volume.shape)
    return (grad_volume, grad_weight)


def solution(mesh):
    return jax.shard_map(
        functools.partial(shards, mesh.shape["space"], mesh.shape["chan"]),
        mesh=mesh,
        in_specs=(
            P(("groups", "space"), "chan", None, None),
            P(None, "space", "chan"),
            P(("groups", "space"), None, None, "chan"),
        ),
        out_specs=(P(("groups", "space"), "chan", None, None), P("groups", "space", "chan")),
        check_vma=False,
    )
```

```python
import functools

import jax
import jax.numpy as jnp
from jax import lax
from jax.experimental import pallas as pl
from jax.experimental.pallas import tpu as pltpu
from jax.sharding import PartitionSpec as P

LANES = 128
TURN_FLOPS = 4 * 10**9
BF16 = jnp.bfloat16
F32 = jnp.float32


def other(me, step):
    return me ^ step


def fetch(x, axis, pairs):
    return lax.ppermute(x, axis, pairs)


def lane_group(shape, width):
    return lax.broadcasted_iota(jnp.int32, shape, len(shape) - 1) // width


def merge(parts, width, flip):
    group = lane_group(parts[0].shape, width)
    out = parts[flip]
    for g in range(1, len(parts)):
        out = jnp.where(group == g, parts[g ^ flip], out)
    return out


def swap_groups(x, width, flip):
    if flip == 0:
        return x
    tiles = []
    for t in range(x.shape[1] // LANES):
        tile = x[:, t * LANES:(t + 1) * LANES]
        bit = 1
        while bit <= flip:
            if flip & bit:
                shift = width * bit
                up = pltpu.roll(tile, LANES - shift, 1)
                if 2 * shift == LANES:
                    tile = up
                else:
                    even = (lane_group(tile.shape, shift) % 2) == 0
                    tile = jnp.where(even, up, pltpu.roll(tile, shift, 1))
            bit *= 2
        tiles.append(tile)
    return tiles[0] if len(tiles) == 1 else jnp.concatenate(tiles, axis=1)


def whole(x):
    return pl.BlockSpec(x.shape, lambda *_: (0,) * len(x.shape))


def params():
    return pltpu.CompilerParams(vmem_limit_bytes=48 * 1024 * 1024)


def cost(flops, bytes_accessed):
    return pl.CostEstimate(flops=flops, bytes_accessed=bytes_accessed, transcendentals=0)


def spread(x, width, at):
    if width >= LANES:
        return x
    zeros = jnp.zeros((x.shape[0], LANES - width), x.dtype)
    full = jnp.concatenate([x, zeros], axis=1)
    return pltpu.roll(full, at * width, 1) if at else full


def pack_weight(weight, ratio):
    kinds, rows, width = weight.shape
    groups = kinds // ratio
    lanes = ratio * width

    def body(w_ref, *outs):
        for g in range(groups):
            for flip in range(ratio):
                acc = None
                for lane in range(ratio):
                    part = spread(w_ref[g * ratio + (lane ^ flip)].astype(F32), width, lane)
                    acc = part if acc is None else acc + part
                outs[flip][g] = acc.astype(BF16)

    return pl.pallas_call(
        body,
        out_shape=[jax.ShapeDtypeStruct((groups, rows, lanes), BF16)] * ratio,
        compiler_params=params(),
        name="pack_weight",
    )(weight)


def pack_cot(cot, chans, after=()):
    planes, cells_y, width, cells_z = cot.shape
    own_y = cells_y // chans

    def body(c_ref, *refs):
        outs = refs[len(after):]
        me = lax.axis_index("chan")
        for step in range(chans):
            target = other(me, step) * own_y
            for p in range(planes):
                for y in range(own_y):
                    outs[step][p * own_y + y] = c_ref[p, target + y]

    return pl.pallas_call(
        body,
        in_specs=[pl.BlockSpec(memory_space=pltpu.VMEM)] + [pl.BlockSpec(memory_space=pl.ANY)] * len(after),
        out_shape=[jax.ShapeDtypeStruct((planes * own_y, width, cells_z), BF16)] * chans,
        compiler_params=params(),
        name="pack_cot",
    )(cot, *after)


def merge_tile(parts, width, after=()):
    groups, block, lanes = parts[0].shape
    ratio = len(parts)

    def body(*refs):
        out = refs[-1]
        for g in range(groups):
            got = [refs[u][g] for u in range(ratio)]
            for q in range(ratio):
                out[g * ratio + q] = merge(got, width, q)

    return pl.pallas_call(
        body,
        in_specs=[pl.BlockSpec(memory_space=pltpu.VMEM)] * ratio + [pl.BlockSpec(memory_space=pl.ANY)] * len(after),
        out_shape=jax.ShapeDtypeStruct((groups * ratio, block, lanes), BF16),
        compiler_params=params(),
        name="merge_tile",
    )(*parts, *after)


def gate(tile, after):
    def body(t_ref, *refs):
        refs[-1][...] = t_ref[...]

    return pl.pallas_call(
        body,
        in_specs=[pl.BlockSpec(memory_space=pltpu.VMEM)] + [pl.BlockSpec(memory_space=pl.ANY)] * len(after),
        out_shape=jax.ShapeDtypeStruct(tile.shape, tile.dtype),
        compiler_params=params(),
        name="gate",
    )(tile, *after)


def patch_rows(volume, after=()):
    cells_x, cells_y, cells_z, in_chan = volume.shape
    nx, ny, nz = cells_x // 2, cells_y // 2, cells_z // 2
    rows = nx * ny * nz

    def body(v_ref, *refs):
        p_ref, t_ref = refs[-2:]
        row = lax.broadcasted_iota(jnp.int32, (cells_z, cells_z), 0)
        col = lax.broadcasted_iota(jnp.int32, (cells_z, cells_z), 1)
        pick = (col == 2 * (row % nz) + row // nz).astype(F32).astype(BF16)
        for n in range(nx * ny):
            here = slice(n * nz, (n + 1) * nz)
            for a in range(2):
                for b in range(2):
                    k = 4 * a + 2 * b
                    got = jnp.dot(pick, v_ref[2 * (n // ny) + a, 2 * (n % ny) + b], preferred_element_type=F32)
                    got = got.astype(BF16)
                    for e in range(2):
                        part = got[e * nz:(e + 1) * nz]
                        p_ref[k + e, here] = part
                        t_ref[k + e, :, here] = part.T

    return pl.pallas_call(
        body,
        in_specs=[pl.BlockSpec(memory_space=pltpu.VMEM)] + [pl.BlockSpec(memory_space=pl.ANY)] * len(after),
        out_shape=[
            jax.ShapeDtypeStruct((8, rows, in_chan), BF16),
            jax.ShapeDtypeStruct((8, in_chan, rows), BF16),
        ],
        compiler_params=params(),
        cost_estimate=cost(16 * rows * in_chan * cells_z, 6 * volume.size),
        name="patch_rows",
    )(volume, *after)


def turn_cot(cots):
    tiles, width, cells = cots[0].shape
    out_chan = width * len(cots)

    def body(*refs):
        out = refs[-1]
        for n in range(tiles):
            column = jnp.concatenate([ref[n] for ref in refs[:-1]], axis=0)
            out[n * cells:(n + 1) * cells] = column.T

    return pl.pallas_call(
        body,
        out_shape=jax.ShapeDtypeStruct((tiles * cells, out_chan), BF16),
        compiler_params=params(),
        cost_estimate=cost(TURN_FLOPS, 4 * tiles * cells * out_chan),
        name="turn_cot",
    )(*cots)


def forward(patches, lines, upstream, width, ratio):
    kinds, rows, in_chan = patches.shape
    _, block, lanes = lines[0][0].shape
    spaces, lane_tiles = len(lines), len(lines[0])
    out_chan = lane_tiles * lanes
    flat = [tile for line in lines for tile in line]

    def body(p_ref, u_ref, *refs):
        ins = refs[:len(flat)]
        d_ref, w_ref = refs[-2:]
        me = lax.axis_index("space")
        for j in range(spaces):
            at = pl.multiple_of(other(me, j) * block, block)
            for t in range(lane_tiles):
                for k in range(kinds):
                    w_ref[k, pl.ds(at, block), t * lanes:(t + 1) * lanes] = ins[j * lane_tiles + t][k]
        part_rows = rows // 2
        for first in range(0, rows, part_rows):
            here = slice(first, first + part_rows)
            pre = None
            for q in range(ratio):
                acc = None
                for k in range(q, kinds, ratio):
                    part = jnp.dot(p_ref[k, here], w_ref[k], preferred_element_type=F32)
                    acc = part if acc is None else acc + part
                acc = swap_groups(acc, width, q)
                pre = acc if pre is None else pre + acc
            up = u_ref[here].astype(F32)
            squash = 1.0 / (1.0 + jnp.exp(-pre))
            slopes = squash * (1.0 + pre * (1.0 - squash))
            delta = (up * slopes).astype(BF16)
            d_ref[0, here] = delta
            for q in range(1, ratio):
                d_ref[q, here] = swap_groups(delta.astype(F32), width, q).astype(BF16)

    return pl.pallas_call(
        body,
        out_shape=[
            jax.ShapeDtypeStruct((ratio, rows, out_chan), BF16),
            jax.ShapeDtypeStruct((kinds, in_chan, out_chan), BF16),
        ],
        compiler_params=params(),
        cost_estimate=cost(2 * patches.size * out_chan, 2 * patches.size),
        name="forward",
    )(patches, upstream, *flat)


def weight_part(turned, deltas, steps, spaces, lanes, dtype):
    kinds, in_chan, rows = turned.shape
    ratio, _, out_chan = deltas.shape
    block = in_chan // spaces
    tiles = out_chan // lanes

    def body(t_ref, d_ref, *outs):
        me = lax.axis_index("space")
        ats = [pl.multiple_of(other(me, step) * block, block) for step in steps]
        for q in range(ratio):
            ks = range(q, kinds, ratio)
            for n, at in enumerate(ats):
                left = jnp.concatenate([t_ref[k, pl.ds(at, block)] for k in ks], axis=0)
                got = jnp.dot(left, d_ref[q], preferred_element_type=F32).astype(dtype)
                for i, k in enumerate(ks):
                    for t in range(tiles):
                        outs[t][n, k] = got[i * block:(i + 1) * block, t * lanes:(t + 1) * lanes]

    return pl.pallas_call(
        body,
        out_shape=[jax.ShapeDtypeStruct((len(steps), kinds, block, lanes), dtype)] * tiles,
        compiler_params=params(),
        cost_estimate=cost(2 * turned.size * out_chan * len(steps) // spaces, 2 * turned.size),
        name="weight_part",
    )(turned, deltas)


def add_core(mine, theirs):
    count, kinds, block, lanes = mine.shape

    def body(a_ref, b_ref, *outs):
        for n in range(count):
            outs[n][...] = (a_ref[n] + b_ref[n].astype(F32)).astype(outs[n].dtype)

    return pl.pallas_call(
        body,
        out_shape=[jax.ShapeDtypeStruct((kinds, block, lanes), BF16 if n else F32) for n in range(count)],
        compiler_params=params(),
        name="add_core",
    )(mine, theirs)


def add_and_pack(mine, theirs, width, after=()):
    kinds, block, lanes = mine.shape
    ratio = lanes // width
    groups = kinds // ratio

    def body(*refs):
        ins, outs = refs[:1 + len(theirs)], refs[1 + len(theirs) + len(after):]
        for g in range(groups):
            sums = []
            for q in range(ratio):
                acc = ins[0][g * ratio + q]
                for ref in ins[1:]:
                    acc = acc + ref[g * ratio + q].astype(F32)
                sums.append(acc)
            for u in range(ratio):
                outs[u][g] = swap_groups(merge(sums, width, u), width, u).astype(BF16)

    return pl.pallas_call(
        body,
        in_specs=[pl.BlockSpec(memory_space=pltpu.VMEM)] * (1 + len(theirs))
        + [pl.BlockSpec(memory_space=pl.ANY)] * len(after),
        out_shape=[jax.ShapeDtypeStruct((groups, block, lanes), BF16)] * ratio,
        compiler_params=params(),
        name="add_and_pack",
    )(mine, *theirs, *after)


def add_core_near(mine, theirs, width, after=()):
    count, kinds, block, lanes = mine.shape
    ratio = lanes // width
    groups = kinds // ratio

    def body(a_ref, b_ref, *refs):
        outs = refs[len(after):]
        for n in range(count):
            for g in range(groups):
                at = n * groups + g
                sums = [
                    a_ref[n, g * ratio + q] + b_ref[n, g * ratio + q].astype(F32) for q in range(ratio)
                ]
                for u in range(ratio):
                    outs[u][at] = swap_groups(merge(sums, width, u), width, u).astype(outs[u].dtype)

    return pl.pallas_call(
        body,
        in_specs=[pl.BlockSpec(memory_space=pltpu.VMEM)] * 2 + [pl.BlockSpec(memory_space=pl.ANY)] * len(after),
        out_shape=[
            jax.ShapeDtypeStruct((count * groups, block, lanes), BF16 if u else F32) for u in range(ratio)
        ],
        compiler_params=params(),
        name="add_core_near",
    )(mine, theirs, *after)


def add_near(mine, theirs, groups, after=()):
    total, block, lanes = mine.shape
    count = total // groups

    def body(*refs):
        ins, outs = refs[:1 + len(theirs)], refs[1 + len(theirs) + len(after):]
        for n in range(count):
            here = slice(n * groups, (n + 1) * groups)
            acc = ins[0][here]
            for ref in ins[1:]:
                acc = acc + ref[here].astype(F32)
            outs[n][...] = acc.astype(outs[n].dtype)

    return pl.pallas_call(
        body,
        in_specs=[pl.BlockSpec(memory_space=pltpu.VMEM)] * (1 + len(theirs))
        + [pl.BlockSpec(memory_space=pl.ANY)] * len(after),
        out_shape=[jax.ShapeDtypeStruct((groups, block, lanes), BF16 if n else F32) for n in range(count)],
        compiler_params=params(),
        name="add_near",
    )(mine, *theirs, *after)


def fold(parts):
    def body(*refs):
        acc = refs[0][...].astype(F32)
        for ref in refs[1:-1]:
            acc = acc + ref[...].astype(F32)
        refs[-1][...] = acc

    return pl.pallas_call(
        body,
        out_shape=jax.ShapeDtypeStruct(parts[0].shape, F32),
        compiler_params=params(),
        name="fold",
    )(*parts)


def finish(parts, kinds, width, scale):
    groups, block, lanes = parts[0].shape
    ratio = lanes // width

    def body(*refs):
        out = refs[-1]
        for g in range(groups):
            acc = refs[0][g]
            for ref in refs[1:-1]:
                acc = acc + ref[g].astype(F32)
            acc = acc * scale
            for q in range(ratio):
                moved = pltpu.roll(acc, lanes - q * width, 1) if q else acc
                out[g * ratio + q] = moved[:, :width]

    return pl.pallas_call(
        body,
        out_shape=jax.ShapeDtypeStruct((kinds, block, width), F32),
        compiler_params=params(),
        name="finish",
    )(*parts)


def volume_grad(deltas, weights, shape):
    cells_x, cells_y, cells_z, in_chan = shape
    nx, ny, nz = cells_x // 2, cells_y // 2, cells_z // 2
    ratio, rows, out_chan = deltas.shape

    def body(d_ref, w_ref, o_ref, mark_ref):
        mark_ref[...] = jnp.zeros_like(mark_ref)
        row = lax.broadcasted_iota(jnp.int32, (cells_z, nz), 0)
        col = lax.broadcasted_iota(jnp.int32, (cells_z, nz), 1)
        wide = {}
        for k in range(8):
            e, q = k % 2, k % ratio
            if (e, q) not in wide:
                put = (row == 2 * col + e).astype(F32).astype(BF16)
                wide[e, q] = jnp.dot(put, d_ref[q], preferred_element_type=F32).astype(BF16)
        for a in range(2):
            for b in range(2):
                acc = None
                for e in range(2):
                    k = 4 * a + 2 * b + e
                    part = lax.dot_general(
                        wide[e, k % ratio], w_ref[k], (((1,), (1,)), ((), ())), preferred_element_type=F32
                    )
                    acc = part if acc is None else acc + part
                o_ref[a, b] = acc.astype(BF16)

    return pl.pallas_call(
        body,
        grid=(nx * ny,),
        in_specs=[pl.BlockSpec((ratio, nz, out_chan), lambda n: (0, n, 0)), whole(weights)],
        out_specs=[
            pl.BlockSpec((2, 2, cells_z, in_chan), lambda n: (n // ny, n % ny, 0, 0)),
            pl.BlockSpec((8, LANES), lambda n: (0, 0)),
        ],
        out_shape=[jax.ShapeDtypeStruct(shape, BF16), jax.ShapeDtypeStruct((8, LANES), F32)],
        compiler_params=params(),
        cost_estimate=cost(32 * rows * in_chan * out_chan, 2 * rows * 8 * in_chan),
        name="volume_grad",
    )(deltas, weights)


def shards(spaces, chans, volume, weight, cotangent):
    kinds, block, width = weight.shape
    ratio = max(1, LANES // width)
    out_rows = volume.shape[0] * volume.shape[1] * volume.shape[2] // 8

    def pairs(count, step):
        return [(d, other(d, step)) for d in range(count)]

    packed = pack_weight(weight, ratio)
    line = [packed[0]] + [fetch(packed[i % ratio], "chan", pairs(chans, i)) for i in range(1, chans)]
    lane_tiles = chans // ratio
    own = [merge_tile(line[t * ratio:(t + 1) * ratio], width) for t in range(lane_tiles)]
    tiles = pack_cot(cotangent.transpose(0, 1, 3, 2), chans, own[:1])
    cots = [tiles[0]] + [fetch(tiles[i], "chan", pairs(chans, i)) for i in range(1, chans)]
    upstream = turn_cot(cots)
    patches, turned = patch_rows(volume, own[1:])
    lines = []
    for j in range(0, spaces, 2):
        lines.append([fetch(tile, "space", pairs(spaces, j)) for tile in own] if j else own)
        lines.append([fetch(gate(tile, (upstream,)) if not j and t else gate(tile, (patches,)) if not j else tile, "space", pairs(spaces, 1)) for t, tile in enumerate(lines[-1])])
    deltas, weights = forward(patches, lines, upstream, width, ratio)
    steps = list(range(0, spaces, 2))
    lanes = ratio * width
    away = weight_part(turned, deltas, [s + 1 for s in steps], spaces, lanes, BF16)
    crossed = [fetch(tile, "space", pairs(spaces, 1)) for tile in away]
    near = weight_part(turned, deltas, steps, spaces, lanes, F32)
    grad_volume, mark = volume_grad(deltas, weights, volume.shape)
    far, outs = [], []
    for t in reversed(range(1, lane_tiles)):
        sums = add_core(near[t], crossed[t])
        far = list(sums[1:]) + far
        came = [fetch(sums[n], "space", pairs(spaces, steps[n])) for n in range(1, len(steps))]
        outs += [(t * ratio + u, part) for u, part in enumerate(add_and_pack(sums[0], came, width, (mark,)))]
    parts = add_core_near(near[0], crossed[0], width, far[:1])
    got = [fetch(parts[u], "chan", pairs(chans, u)) for u in range(1, ratio)]
    sums = add_near(parts[0], got, kinds // ratio, [part for _, part in outs[-1:]])
    got = [sums[0]] + [fetch(sums[n], "space", pairs(spaces, steps[n])) for n in range(1, len(steps))]
    spread_out = [fetch(part, "chan", pairs(chans, i)) for i, part in outs]
    got += [fold(spread_out)] if spread_out else []
    grad_weight = finish(got, kinds, width, 1.0 / out_rows)
    return (grad_volume, grad_weight)


def solution(mesh):
    return jax.shard_map(
        functools.partial(shards, mesh.shape["space"], mesh.shape["chan"]),
        mesh=mesh,
        in_specs=(
            P(("groups", "space"), "chan", None, None),
            P(None, "space", "chan"),
            P(("groups", "space"), None, None, "chan"),
        ),
        out_specs=(P(("groups", "space"), "chan", None, None), P("groups", "space", "chan")),
        check_vma=False,
    )
```

```python
import functools

import jax
import jax.numpy as jnp
from jax import lax
from jax.experimental import pallas as pl
from jax.experimental.pallas import tpu as pltpu
from jax.sharding import PartitionSpec as P

LANES = 128
TURN_FLOPS = 4 * 10**9
BF16 = jnp.bfloat16
F32 = jnp.float32


def other(me, step):
    return me ^ step


def fetch(x, axis, pairs):
    return lax.ppermute(x, axis, pairs)


def lane_group(shape, width):
    return lax.broadcasted_iota(jnp.int32, shape, len(shape) - 1) // width


def merge(parts, width, flip):
    group = lane_group(parts[0].shape, width)
    out = parts[flip]
    for g in range(1, len(parts)):
        out = jnp.where(group == g, parts[g ^ flip], out)
    return out


def swap_groups(x, width, flip):
    if flip == 0:
        return x
    tiles = []
    for t in range(x.shape[1] // LANES):
        tile = x[:, t * LANES:(t + 1) * LANES]
        bit = 1
        while bit <= flip:
            if flip & bit:
                shift = width * bit
                up = pltpu.roll(tile, LANES - shift, 1)
                if 2 * shift == LANES:
                    tile = up
                else:
                    even = (lane_group(tile.shape, shift) % 2) == 0
                    tile = jnp.where(even, up, pltpu.roll(tile, shift, 1))
            bit *= 2
        tiles.append(tile)
    return tiles[0] if len(tiles) == 1 else jnp.concatenate(tiles, axis=1)


def whole(x):
    return pl.BlockSpec(x.shape, lambda *_: (0,) * len(x.shape))


def params():
    return pltpu.CompilerParams(vmem_limit_bytes=48 * 1024 * 1024)


def cost(flops, bytes_accessed):
    return pl.CostEstimate(flops=flops, bytes_accessed=bytes_accessed, transcendentals=0)


def spread(x, width, at):
    if width >= LANES:
        return x
    zeros = jnp.zeros((x.shape[0], LANES - width), x.dtype)
    full = jnp.concatenate([x, zeros], axis=1)
    return pltpu.roll(full, at * width, 1) if at else full


def pack_weight(weight, ratio):
    kinds, rows, width = weight.shape
    groups = kinds // ratio
    lanes = ratio * width

    def body(w_ref, *outs):
        for g in range(groups):
            for flip in range(ratio):
                acc = None
                for lane in range(ratio):
                    part = spread(w_ref[g * ratio + (lane ^ flip)].astype(F32), width, lane)
                    acc = part if acc is None else acc + part
                outs[flip][g] = acc.astype(BF16)

    return pl.pallas_call(
        body,
        out_shape=[jax.ShapeDtypeStruct((groups, rows, lanes), BF16)] * ratio,
        compiler_params=params(),
        name="pack_weight",
    )(weight)


def pack_cot(cot, chans, after=()):
    planes, cells_y, width, cells_z = cot.shape
    own_y = cells_y // chans

    def body(c_ref, *refs):
        outs = refs[len(after):]
        me = lax.axis_index("chan")
        for step in range(chans):
            target = other(me, step) * own_y
            for p in range(planes):
                for y in range(own_y):
                    outs[step][p * own_y + y] = c_ref[p, target + y]

    return pl.pallas_call(
        body,
        in_specs=[pl.BlockSpec(memory_space=pltpu.VMEM)] + [pl.BlockSpec(memory_space=pl.ANY)] * len(after),
        out_shape=[jax.ShapeDtypeStruct((planes * own_y, width, cells_z), BF16)] * chans,
        compiler_params=params(),
        name="pack_cot",
    )(cot, *after)


def merge_tile(parts, width, after=()):
    groups, block, lanes = parts[0].shape
    ratio = len(parts)

    def body(*refs):
        out = refs[-1]
        for g in range(groups):
            got = [refs[u][g] for u in range(ratio)]
            for q in range(ratio):
                out[g * ratio + q] = merge(got, width, q)

    return pl.pallas_call(
        body,
        in_specs=[pl.BlockSpec(memory_space=pltpu.VMEM)] * ratio + [pl.BlockSpec(memory_space=pl.ANY)] * len(after),
        out_shape=jax.ShapeDtypeStruct((groups * ratio, block, lanes), BF16),
        compiler_params=params(),
        name="merge_tile",
    )(*parts, *after)


def gate(tile, after):
    def body(t_ref, *refs):
        refs[-1][...] = t_ref[...]

    return pl.pallas_call(
        body,
        in_specs=[pl.BlockSpec(memory_space=pltpu.VMEM)] + [pl.BlockSpec(memory_space=pl.ANY)] * len(after),
        out_shape=jax.ShapeDtypeStruct(tile.shape, tile.dtype),
        compiler_params=params(),
        name="gate",
    )(tile, *after)


def patch_rows(volume, after=()):
    cells_x, cells_y, cells_z, in_chan = volume.shape
    nx, ny, nz = cells_x // 2, cells_y // 2, cells_z // 2
    rows = nx * ny * nz

    def body(v_ref, *refs):
        p_ref, t_ref = refs[-2:]
        row = lax.broadcasted_iota(jnp.int32, (cells_z, cells_z), 0)
        col = lax.broadcasted_iota(jnp.int32, (cells_z, cells_z), 1)
        pick = (col == 2 * (row % nz) + row // nz).astype(F32).astype(BF16)
        for n in range(nx * ny):
            here = slice(n * nz, (n + 1) * nz)
            for a in range(2):
                for b in range(2):
                    k = 4 * a + 2 * b
                    got = jnp.dot(pick, v_ref[2 * (n // ny) + a, 2 * (n % ny) + b], preferred_element_type=F32)
                    got = got.astype(BF16)
                    for e in range(2):
                        part = got[e * nz:(e + 1) * nz]
                        p_ref[k + e, here] = part
                        t_ref[k + e, :, here] = part.T

    return pl.pallas_call(
        body,
        in_specs=[pl.BlockSpec(memory_space=pltpu.VMEM)] + [pl.BlockSpec(memory_space=pl.ANY)] * len(after),
        out_shape=[
            jax.ShapeDtypeStruct((8, rows, in_chan), BF16),
            jax.ShapeDtypeStruct((8, in_chan, rows), BF16),
        ],
        compiler_params=params(),
        cost_estimate=cost(16 * rows * in_chan * cells_z, 6 * volume.size),
        name="patch_rows",
    )(volume, *after)


def turn_cot(cots):
    tiles, width, cells = cots[0].shape
    out_chan = width * len(cots)

    def body(*refs):
        out = refs[-1]
        for n in range(tiles):
            column = jnp.concatenate([ref[n] for ref in refs[:-1]], axis=0)
            out[n * cells:(n + 1) * cells] = column.T

    return pl.pallas_call(
        body,
        out_shape=jax.ShapeDtypeStruct((tiles * cells, out_chan), BF16),
        compiler_params=params(),
        cost_estimate=cost(TURN_FLOPS, 4 * tiles * cells * out_chan),
        name="turn_cot",
    )(*cots)


def place(w_ref, ins, me, first, tiles):
    kinds, block, lanes = ins[0].shape
    for n in range(len(ins) // tiles):
        at = pl.multiple_of(other(me, first + n) * block, block)
        for t in range(tiles):
            for k in range(kinds):
                w_ref[k, pl.ds(at, block), t * lanes:(t + 1) * lanes] = ins[n * tiles + t][k]


def chip_part(p_ref, w_ref, here, me, chip, block, ratio, q):
    kinds = w_ref.shape[0]
    span = 2 * block
    at = pl.multiple_of(other(me, chip) // 2 * span, span)
    ks = range(q, kinds, ratio)
    per = max(1, min(len(ks), w_ref.shape[1] // span))
    acc = None
    for first in range(0, len(ks), per):
        some = ks[first:first + per]
        left = jnp.concatenate([p_ref[k, here, pl.ds(at, span)] for k in some], axis=1)
        right = jnp.concatenate([w_ref[k, pl.ds(at, span)] for k in some], axis=0)
        part = jnp.dot(left, right, preferred_element_type=F32)
        acc = part if acc is None else acc + part
    return acc


def forward_own(patches, lines, spaces, width, ratio):
    kinds, rows, in_chan = patches.shape
    _, block, lanes = lines[0][0].shape
    tiles = len(lines[0])
    out_chan = tiles * lanes
    flat = [tile for line in lines for tile in line]

    def body(p_ref, *refs):
        pre_ref, w_ref = refs[-2:]
        me = lax.axis_index("space")
        place(w_ref, refs[:-2], me, 0, tiles)
        for first in range(0, rows, rows // 2):
            here = slice(first, first + rows // 2)
            pre = None
            for q in range(ratio):
                acc = swap_groups(chip_part(p_ref, w_ref, here, me, 0, block, ratio, q), width, q)
                pre = acc if pre is None else pre + acc
            pre_ref[here] = pre

    return pl.pallas_call(
        body,
        out_shape=[
            jax.ShapeDtypeStruct((rows, out_chan), F32),
            jax.ShapeDtypeStruct((kinds, in_chan, out_chan), BF16),
        ],
        compiler_params=params(),
        cost_estimate=cost(4 * patches.size * out_chan // spaces, 2 * patches.size),
        name="forward_own",
    )(patches, *flat)


def forward(patches, own, lines, upstream, width, ratio):
    kinds, rows, in_chan = patches.shape
    tiles = len(lines[0])
    _, block, lanes = lines[0][0].shape
    out_chan = tiles * lanes
    spaces = len(lines)
    start = 0 if own is None else 2
    flat = [tile for line in lines[start:] for tile in line]

    def body(p_ref, u_ref, *refs):
        d_ref, w_ref = refs[-2:]
        me = lax.axis_index("space")
        place(w_ref, refs[:len(flat)], me, start, tiles)
        for first in range(0, rows, rows // 2):
            here = slice(first, first + rows // 2)
            pre = None if own is None else refs[len(flat)][here]
            for q in range(ratio):
                acc = None
                if own is None:
                    for k in range(q, kinds, ratio):
                        part = jnp.dot(p_ref[k, here], w_ref[k], preferred_element_type=F32)
                        acc = part if acc is None else acc + part
                else:
                    for chip in range(start, spaces, 2):
                        part = chip_part(p_ref, w_ref, here, me, chip, block, ratio, q)
                        acc = part if acc is None else acc + part
                acc = swap_groups(acc, width, q)
                pre = acc if pre is None else pre + acc
            up = u_ref[here].astype(F32)
            squash = 1.0 / (1.0 + jnp.exp(-pre))
            slopes = squash * (1.0 + pre * (1.0 - squash))
            delta = (up * slopes).astype(BF16)
            d_ref[0, here] = delta
            for q in range(1, ratio):
                d_ref[q, here] = swap_groups(delta.astype(F32), width, q).astype(BF16)

    extra = () if own is None else own
    return pl.pallas_call(
        body,
        out_shape=[
            jax.ShapeDtypeStruct((ratio, rows, out_chan), BF16),
            jax.ShapeDtypeStruct((kinds, in_chan, out_chan), BF16),
        ],
        input_output_aliases={} if own is None else {2 + len(flat) + 1: 1},
        compiler_params=params(),
        cost_estimate=cost(2 * patches.size * out_chan, 2 * patches.size),
        name="forward",
    )(patches, upstream, *flat, *extra)


def weight_part(turned, deltas, steps, spaces, lanes, dtype):
    kinds, in_chan, rows = turned.shape
    ratio, _, out_chan = deltas.shape
    block = in_chan // spaces
    tiles = out_chan // lanes

    def body(t_ref, d_ref, *outs):
        me = lax.axis_index("space")
        ats = [pl.multiple_of(other(me, step) * block, block) for step in steps]
        for q in range(ratio):
            ks = range(q, kinds, ratio)
            for n, at in enumerate(ats):
                left = jnp.concatenate([t_ref[k, pl.ds(at, block)] for k in ks], axis=0)
                got = jnp.dot(left, d_ref[q], preferred_element_type=F32).astype(dtype)
                for i, k in enumerate(ks):
                    for t in range(tiles):
                        outs[t][n, k] = got[i * block:(i + 1) * block, t * lanes:(t + 1) * lanes]

    return pl.pallas_call(
        body,
        out_shape=[jax.ShapeDtypeStruct((len(steps), kinds, block, lanes), dtype)] * tiles,
        compiler_params=params(),
        cost_estimate=cost(2 * turned.size * out_chan * len(steps) // spaces, 2 * turned.size),
        name="weight_part",
    )(turned, deltas)


def add_core(mine, theirs):
    count, kinds, block, lanes = mine.shape

    def body(a_ref, b_ref, *outs):
        for n in range(count):
            outs[n][...] = (a_ref[n] + b_ref[n].astype(F32)).astype(outs[n].dtype)

    return pl.pallas_call(
        body,
        out_shape=[jax.ShapeDtypeStruct((kinds, block, lanes), BF16 if n else F32) for n in range(count)],
        compiler_params=params(),
        name="add_core",
    )(mine, theirs)


def add_and_pack(mine, theirs, width, after=()):
    kinds, block, lanes = mine.shape
    ratio = lanes // width
    groups = kinds // ratio

    def body(*refs):
        ins, outs = refs[:1 + len(theirs)], refs[1 + len(theirs) + len(after):]
        for g in range(groups):
            sums = []
            for q in range(ratio):
                acc = ins[0][g * ratio + q]
                for ref in ins[1:]:
                    acc = acc + ref[g * ratio + q].astype(F32)
                sums.append(acc)
            for u in range(ratio):
                outs[u][g] = swap_groups(merge(sums, width, u), width, u).astype(BF16)

    return pl.pallas_call(
        body,
        in_specs=[pl.BlockSpec(memory_space=pltpu.VMEM)] * (1 + len(theirs))
        + [pl.BlockSpec(memory_space=pl.ANY)] * len(after),
        out_shape=[jax.ShapeDtypeStruct((groups, block, lanes), BF16)] * ratio,
        compiler_params=params(),
        name="add_and_pack",
    )(mine, *theirs, *after)


def add_core_near(mine, theirs, width, after=()):
    count, kinds, block, lanes = mine.shape
    ratio = lanes // width
    groups = kinds // ratio

    def body(a_ref, b_ref, *refs):
        outs = refs[len(after):]
        for n in range(count):
            for g in range(groups):
                at = n * groups + g
                sums = [
                    a_ref[n, g * ratio + q] + b_ref[n, g * ratio + q].astype(F32) for q in range(ratio)
                ]
                for u in range(ratio):
                    outs[u][at] = swap_groups(merge(sums, width, u), width, u).astype(outs[u].dtype)

    return pl.pallas_call(
        body,
        in_specs=[pl.BlockSpec(memory_space=pltpu.VMEM)] * 2 + [pl.BlockSpec(memory_space=pl.ANY)] * len(after),
        out_shape=[
            jax.ShapeDtypeStruct((count * groups, block, lanes), BF16 if u else F32) for u in range(ratio)
        ],
        compiler_params=params(),
        name="add_core_near",
    )(mine, theirs, *after)


def add_near(mine, theirs, groups, after=()):
    total, block, lanes = mine.shape
    count = total // groups

    def body(*refs):
        ins, outs = refs[:1 + len(theirs)], refs[1 + len(theirs) + len(after):]
        for n in range(count):
            here = slice(n * groups, (n + 1) * groups)
            acc = ins[0][here]
            for ref in ins[1:]:
                acc = acc + ref[here].astype(F32)
            outs[n][...] = acc.astype(outs[n].dtype)

    return pl.pallas_call(
        body,
        in_specs=[pl.BlockSpec(memory_space=pltpu.VMEM)] * (1 + len(theirs))
        + [pl.BlockSpec(memory_space=pl.ANY)] * len(after),
        out_shape=[jax.ShapeDtypeStruct((groups, block, lanes), BF16 if n else F32) for n in range(count)],
        compiler_params=params(),
        name="add_near",
    )(mine, *theirs, *after)


def fold(parts):
    def body(*refs):
        acc = refs[0][...].astype(F32)
        for ref in refs[1:-1]:
            acc = acc + ref[...].astype(F32)
        refs[-1][...] = acc

    return pl.pallas_call(
        body,
        out_shape=jax.ShapeDtypeStruct(parts[0].shape, F32),
        compiler_params=params(),
        name="fold",
    )(*parts)


def finish(parts, kinds, width, scale):
    groups, block, lanes = parts[0].shape
    ratio = lanes // width

    def body(*refs):
        out = refs[-1]
        for g in range(groups):
            acc = refs[0][g]
            for ref in refs[1:-1]:
                acc = acc + ref[g].astype(F32)
            acc = acc * scale
            for q in range(ratio):
                moved = pltpu.roll(acc, lanes - q * width, 1) if q else acc
                out[g * ratio + q] = moved[:, :width]

    return pl.pallas_call(
        body,
        out_shape=jax.ShapeDtypeStruct((kinds, block, width), F32),
        compiler_params=params(),
        name="finish",
    )(*parts)


def volume_grad(deltas, weights, shape):
    cells_x, cells_y, cells_z, in_chan = shape
    nx, ny, nz = cells_x // 2, cells_y // 2, cells_z // 2
    ratio, rows, out_chan = deltas.shape
    planes = cells_x * cells_y

    def body(d_ref, w_ref, o_hbm, mark_ref, wide_ref, plane_ref, sem):
        mark_ref[...] = jnp.zeros_like(mark_ref)
        row = lax.broadcasted_iota(jnp.int32, (cells_z, nz), 0)
        col = lax.broadcasted_iota(jnp.int32, (cells_z, nz), 1)
        places = sorted({(k % 2, k % ratio) for k in range(8)})
        for n, (e, q) in enumerate(places):
            put = (row == 2 * col + e).astype(F32).astype(BF16)
            for m in range(nx * ny):
                got = jnp.dot(put, d_ref[q, m * nz:(m + 1) * nz], preferred_element_type=F32)
                wide_ref[n, m * cells_z:(m + 1) * cells_z] = got.astype(BF16)
        moves = []
        for a in range(2):
            for b in range(2):
                acc = None
                for e in range(2):
                    k = 4 * a + 2 * b + e
                    part = lax.dot_general(
                        wide_ref[places.index((e, k % ratio))], w_ref[k], (((1,), (1,)), ((), ())),
                        preferred_element_type=F32,
                    )
                    acc = part if acc is None else acc + part
                out = acc.astype(BF16)
                for m in range(nx * ny):
                    x, y = 2 * (m // ny) + a, 2 * (m % ny) + b
                    at = len(moves)
                    plane_ref[at] = out[m * cells_z:(m + 1) * cells_z]
                    move = pltpu.make_async_copy(plane_ref.at[at], o_hbm.at[x, y], sem.at[at])
                    move.start()
                    moves.append(move)
        for move in moves:
            move.wait()

    return pl.pallas_call(
        body,
        in_specs=[pl.BlockSpec(memory_space=pltpu.VMEM)] * 2,
        out_specs=[pl.BlockSpec(memory_space=pl.ANY), pl.BlockSpec(memory_space=pltpu.VMEM)],
        out_shape=[jax.ShapeDtypeStruct(shape, BF16), jax.ShapeDtypeStruct((8, LANES), F32)],
        scratch_shapes=[
            pltpu.VMEM((max(2, ratio), 4 * rows // 2, out_chan), BF16),
            pltpu.VMEM((planes, cells_z, in_chan), BF16),
            pltpu.SemaphoreType.DMA((planes,)),
        ],
        compiler_params=params(),
        cost_estimate=cost(32 * rows * in_chan * out_chan, 2 * rows * 8 * in_chan),
        name="volume_grad",
    )(deltas, weights)


def shards(spaces, chans, volume, weight, cotangent):
    kinds, block, width = weight.shape
    ratio = max(1, LANES // width)
    out_rows = volume.shape[0] * volume.shape[1] * volume.shape[2] // 8

    def pairs(count, step):
        return [(d, other(d, step)) for d in range(count)]

    packed = pack_weight(weight, ratio)
    line = [packed[0]] + [fetch(packed[i % ratio], "chan", pairs(chans, i)) for i in range(1, chans)]
    lane_tiles = chans // ratio
    own = [merge_tile(line[t * ratio:(t + 1) * ratio], width) for t in range(lane_tiles)]
    tiles = pack_cot(cotangent.transpose(0, 1, 3, 2), chans, own[:1])
    cots = [tiles[0]] + [fetch(tiles[i], "chan", pairs(chans, i)) for i in range(1, chans)]
    upstream = turn_cot(cots)
    patches, turned = patch_rows(volume, own[1:])
    lines = []
    for j in range(0, spaces, 2):
        lines.append([fetch(tile, "space", pairs(spaces, j)) for tile in own] if j else own)
        lines.append([fetch(gate(tile, (patches,)) if not j and not t else gate(tile, (patches,)) if not j else gate(tile, (upstream,)) if not t else gate(tile, (upstream,)), "space", pairs(spaces, 1)) for t, tile in enumerate(lines[-1])])
    own_part = None
    if 2 * block % LANES == 0 and spaces > 2:
        own_part = forward_own(patches, lines[:2], spaces, width, ratio)
    deltas, weights = forward(patches, own_part, lines, upstream, width, ratio)
    steps = list(range(0, spaces, 2))
    lanes = ratio * width
    away = weight_part(turned, deltas, [s + 1 for s in steps], spaces, lanes, BF16)
    crossed = [fetch(tile, "space", pairs(spaces, 1)) for tile in away]
    near = weight_part(turned, deltas, steps, spaces, lanes, F32)
    grad_volume, mark = volume_grad(deltas, weights, volume.shape)
    far, outs = [], []
    for t in reversed(range(1, lane_tiles)):
        sums = add_core(near[t], crossed[t])
        far = list(sums[1:]) + far
        came = [fetch(sums[n], "space", pairs(spaces, steps[n])) for n in range(1, len(steps))]
        outs += [(t * ratio + u, part) for u, part in enumerate(add_and_pack(sums[0], came, width, (mark,)))]
    parts = add_core_near(near[0], crossed[0], width, far[:1])
    got = [fetch(parts[u], "chan", pairs(chans, u)) for u in range(1, ratio)]
    sums = add_near(parts[0], got, kinds // ratio, [part for _, part in outs[-1:]])
    got = [sums[0]] + [fetch(sums[n], "space", pairs(spaces, steps[n])) for n in range(1, len(steps))]
    spread_out = [fetch(part, "chan", pairs(chans, i)) for i, part in outs]
    got += [fold(spread_out)] if spread_out else []
    grad_weight = finish(got, kinds, width, 1.0 / out_rows)
    return (grad_volume, grad_weight)


def solution(mesh):
    return jax.shard_map(
        functools.partial(shards, mesh.shape["space"], mesh.shape["chan"]),
        mesh=mesh,
        in_specs=(
            P(("groups", "space"), "chan", None, None),
            P(None, "space", "chan"),
            P(("groups", "space"), None, None, "chan"),
        ),
        out_specs=(P(("groups", "space"), "chan", None, None), P("groups", "space", "chan")),
        check_vma=False,
    )
```

```python
import functools

import jax
import jax.numpy as jnp
from jax import lax
from jax.experimental import pallas as pl
from jax.experimental.pallas import tpu as pltpu
from jax.sharding import PartitionSpec as P

LANES = 128
TURN_FLOPS = 4 * 10**9
BF16 = jnp.bfloat16
F32 = jnp.float32


def other(me, step):
    return me ^ step


def fetch(x, axis, pairs):
    return lax.ppermute(x, axis, pairs)


def lane_group(shape, width):
    return lax.broadcasted_iota(jnp.int32, shape, len(shape) - 1) // width


def merge(parts, width, flip):
    group = lane_group(parts[0].shape, width)
    out = parts[flip]
    for g in range(1, len(parts)):
        out = jnp.where(group == g, parts[g ^ flip], out)
    return out


def swap_groups(x, width, flip):
    if flip == 0:
        return x
    tiles = []
    for t in range(x.shape[1] // LANES):
        tile = x[:, t * LANES:(t + 1) * LANES]
        bit = 1
        while bit <= flip:
            if flip & bit:
                shift = width * bit
                up = pltpu.roll(tile, LANES - shift, 1)
                if 2 * shift == LANES:
                    tile = up
                else:
                    even = (lane_group(tile.shape, shift) % 2) == 0
                    tile = jnp.where(even, up, pltpu.roll(tile, shift, 1))
            bit *= 2
        tiles.append(tile)
    return tiles[0] if len(tiles) == 1 else jnp.concatenate(tiles, axis=1)


def whole(x):
    return pl.BlockSpec(x.shape, lambda *_: (0,) * len(x.shape))


def params():
    return pltpu.CompilerParams(vmem_limit_bytes=48 * 1024 * 1024)


def cost(flops, bytes_accessed):
    return pl.CostEstimate(flops=flops, bytes_accessed=bytes_accessed, transcendentals=0)


def spread(x, width, at):
    if width >= LANES:
        return x
    zeros = jnp.zeros((x.shape[0], LANES - width), x.dtype)
    full = jnp.concatenate([x, zeros], axis=1)
    return pltpu.roll(full, at * width, 1) if at else full


def pack_weight(weight, ratio):
    kinds, rows, width = weight.shape
    groups = kinds // ratio
    lanes = ratio * width

    def body(w_ref, *outs):
        for g in range(groups):
            for flip in range(ratio):
                acc = None
                for lane in range(ratio):
                    part = spread(w_ref[g * ratio + (lane ^ flip)].astype(F32), width, lane)
                    acc = part if acc is None else acc + part
                outs[flip][g] = acc.astype(BF16)

    return pl.pallas_call(
        body,
        out_shape=[jax.ShapeDtypeStruct((groups, rows, lanes), BF16)] * ratio,
        compiler_params=params(),
        name="pack_weight",
    )(weight)


def pack_cot(cot, chans, after=()):
    planes, cells_y, width, cells_z = cot.shape
    own_y = cells_y // chans

    def body(c_ref, *refs):
        outs = refs[len(after):]
        me = lax.axis_index("chan")
        for step in range(chans):
            target = other(me, step) * own_y
            for p in range(planes):
                for y in range(own_y):
                    outs[step][p * own_y + y] = c_ref[p, target + y]

    return pl.pallas_call(
        body,
        in_specs=[pl.BlockSpec(memory_space=pltpu.VMEM)] + [pl.BlockSpec(memory_space=pl.ANY)] * len(after),
        out_shape=[jax.ShapeDtypeStruct((planes * own_y, width, cells_z), BF16)] * chans,
        compiler_params=params(),
        name="pack_cot",
    )(cot, *after)


def merge_tile(parts, width, after=()):
    groups, block, lanes = parts[0].shape
    ratio = len(parts)

    def body(*refs):
        out = refs[-1]
        for g in range(groups):
            got = [refs[u][g] for u in range(ratio)]
            for q in range(ratio):
                out[g * ratio + q] = merge(got, width, q)

    return pl.pallas_call(
        body,
        in_specs=[pl.BlockSpec(memory_space=pltpu.VMEM)] * ratio + [pl.BlockSpec(memory_space=pl.ANY)] * len(after),
        out_shape=jax.ShapeDtypeStruct((groups * ratio, block, lanes), BF16),
        compiler_params=params(),
        name="merge_tile",
    )(*parts, *after)


def gate(tile, after):
    def body(t_ref, *refs):
        refs[-1][...] = t_ref[...]

    return pl.pallas_call(
        body,
        in_specs=[pl.BlockSpec(memory_space=pltpu.VMEM)] + [pl.BlockSpec(memory_space=pl.ANY)] * len(after),
        out_shape=jax.ShapeDtypeStruct(tile.shape, tile.dtype),
        compiler_params=params(),
        name="gate",
    )(tile, *after)


def patch_rows(volume, after=()):
    cells_x, cells_y, cells_z, in_chan = volume.shape
    nx, ny, nz = cells_x // 2, cells_y // 2, cells_z // 2
    rows = nx * ny * nz

    def body(v_ref, *refs):
        p_ref, t_ref = refs[-2:]
        row = lax.broadcasted_iota(jnp.int32, (cells_z, cells_z), 0)
        col = lax.broadcasted_iota(jnp.int32, (cells_z, cells_z), 1)
        pick = (col == 2 * (row % nz) + row // nz).astype(F32).astype(BF16)
        for n in range(nx * ny):
            here = slice(n * nz, (n + 1) * nz)
            for a in range(2):
                for b in range(2):
                    k = 4 * a + 2 * b
                    got = jnp.dot(pick, v_ref[2 * (n // ny) + a, 2 * (n % ny) + b], preferred_element_type=F32)
                    got = got.astype(BF16)
                    for e in range(2):
                        part = got[e * nz:(e + 1) * nz]
                        p_ref[k + e, here] = part
                        t_ref[k + e, :, here] = part.T

    return pl.pallas_call(
        body,
        in_specs=[pl.BlockSpec(memory_space=pltpu.VMEM)] + [pl.BlockSpec(memory_space=pl.ANY)] * len(after),
        out_shape=[
            jax.ShapeDtypeStruct((8, rows, in_chan), BF16),
            jax.ShapeDtypeStruct((8, in_chan, rows), BF16),
        ],
        compiler_params=params(),
        cost_estimate=cost(16 * rows * in_chan * cells_z, 6 * volume.size),
        name="patch_rows",
    )(volume, *after)


def turn_cot(cots):
    tiles, width, cells = cots[0].shape
    out_chan = width * len(cots)

    def body(*refs):
        out = refs[-1]
        for n in range(tiles):
            column = jnp.concatenate([ref[n] for ref in refs[:-1]], axis=0)
            out[n * cells:(n + 1) * cells] = column.T

    return pl.pallas_call(
        body,
        out_shape=jax.ShapeDtypeStruct((tiles * cells, out_chan), BF16),
        compiler_params=params(),
        cost_estimate=cost(TURN_FLOPS, 4 * tiles * cells * out_chan),
        name="turn_cot",
    )(*cots)


def place(w_ref, ins, me, first, tiles):
    kinds, block, lanes = ins[0].shape
    for n in range(len(ins) // tiles):
        at = pl.multiple_of(other(me, first + n) * block, block)
        for t in range(tiles):
            for k in range(kinds):
                w_ref[k, pl.ds(at, block), t * lanes:(t + 1) * lanes] = ins[n * tiles + t][k]


def chip_part(p_ref, w_ref, here, me, chip, block, ratio, q):
    kinds = w_ref.shape[0]
    span = 2 * block
    at = pl.multiple_of(other(me, chip) // 2 * span, span)
    ks = range(q, kinds, ratio)
    per = max(1, min(len(ks), w_ref.shape[1] // span))
    acc = None
    for first in range(0, len(ks), per):
        some = ks[first:first + per]
        left = jnp.concatenate([p_ref[k, here, pl.ds(at, span)] for k in some], axis=1)
        right = jnp.concatenate([w_ref[k, pl.ds(at, span)] for k in some], axis=0)
        part = jnp.dot(left, right, preferred_element_type=F32)
        acc = part if acc is None else acc + part
    return acc


def forward_own(patches, lines, spaces, width, ratio):
    kinds, rows, in_chan = patches.shape
    _, block, lanes = lines[0][0].shape
    tiles = len(lines[0])
    out_chan = tiles * lanes
    flat = [tile for line in lines for tile in line]

    def body(p_ref, *refs):
        pre_ref, w_ref = refs[-2:]
        me = lax.axis_index("space")
        place(w_ref, refs[:-2], me, 0, tiles)
        for first in range(0, rows, rows // 2):
            here = slice(first, first + rows // 2)
            pre = None
            for q in range(ratio):
                acc = swap_groups(chip_part(p_ref, w_ref, here, me, 0, block, ratio, q), width, q)
                pre = acc if pre is None else pre + acc
            pre_ref[here] = pre

    return pl.pallas_call(
        body,
        out_shape=[
            jax.ShapeDtypeStruct((rows, out_chan), F32),
            jax.ShapeDtypeStruct((kinds, in_chan, out_chan), BF16),
        ],
        compiler_params=params(),
        cost_estimate=cost(4 * patches.size * out_chan // spaces, 2 * patches.size),
        name="forward_own",
    )(patches, *flat)


def forward(patches, own, lines, upstream, width, ratio):
    kinds, rows, in_chan = patches.shape
    tiles = len(lines[0])
    _, block, lanes = lines[0][0].shape
    out_chan = tiles * lanes
    spaces = len(lines)
    start = 0 if own is None else 2
    flat = [tile for line in lines[start:] for tile in line]

    def body(p_ref, u_ref, *refs):
        d_ref, w_ref = refs[-2:]
        me = lax.axis_index("space")
        place(w_ref, refs[:len(flat)], me, start, tiles)
        for first in range(0, rows, rows // 4):
            here = slice(first, first + rows // 4)
            pre = None if own is None else refs[len(flat)][here]
            for q in range(ratio):
                acc = None
                if own is None:
                    for k in range(q, kinds, ratio):
                        part = jnp.dot(p_ref[k, here], w_ref[k], preferred_element_type=F32)
                        acc = part if acc is None else acc + part
                else:
                    for chip in range(start, spaces, 2):
                        part = chip_part(p_ref, w_ref, here, me, chip, block, ratio, q)
                        acc = part if acc is None else acc + part
                acc = swap_groups(acc, width, q)
                pre = acc if pre is None else pre + acc
            up = u_ref[here].astype(F32)
            squash = 1.0 / (1.0 + jnp.exp(-pre))
            slopes = squash * (1.0 + pre * (1.0 - squash))
            delta = (up * slopes).astype(BF16)
            d_ref[0, here] = delta
            for q in range(1, ratio):
                d_ref[q, here] = swap_groups(delta.astype(F32), width, q).astype(BF16)

    extra = () if own is None else own
    return pl.pallas_call(
        body,
        out_shape=[
            jax.ShapeDtypeStruct((ratio, rows, out_chan), BF16),
            jax.ShapeDtypeStruct((kinds, in_chan, out_chan), BF16),
        ],
        input_output_aliases={} if own is None else {2 + len(flat) + 1: 1},
        compiler_params=params(),
        cost_estimate=cost(2 * patches.size * out_chan, 2 * patches.size),
        name="forward",
    )(patches, upstream, *flat, *extra)


def weight_part(turned, deltas, steps, spaces, lanes, dtype):
    kinds, in_chan, rows = turned.shape
    ratio, _, out_chan = deltas.shape
    block = in_chan // spaces
    tiles = out_chan // lanes

    def body(t_ref, d_ref, *outs):
        me = lax.axis_index("space")
        ats = [pl.multiple_of(other(me, step) * block, block) for step in steps]
        for q in range(ratio):
            ks = range(q, kinds, ratio)
            for n, at in enumerate(ats):
                left = jnp.concatenate([t_ref[k, pl.ds(at, block)] for k in ks], axis=0)
                got = jnp.dot(left, d_ref[q], preferred_element_type=F32).astype(dtype)
                for i, k in enumerate(ks):
                    for t in range(tiles):
                        outs[t][n, k] = got[i * block:(i + 1) * block, t * lanes:(t + 1) * lanes]

    return pl.pallas_call(
        body,
        out_shape=[jax.ShapeDtypeStruct((len(steps), kinds, block, lanes), dtype)] * tiles,
        compiler_params=params(),
        cost_estimate=cost(2 * turned.size * out_chan * len(steps) // spaces, 2 * turned.size),
        name="weight_part",
    )(turned, deltas)


def add_core(mine, theirs):
    count, kinds, block, lanes = mine.shape

    def body(a_ref, b_ref, *outs):
        for n in range(count):
            outs[n][...] = (a_ref[n] + b_ref[n].astype(F32)).astype(outs[n].dtype)

    return pl.pallas_call(
        body,
        out_shape=[jax.ShapeDtypeStruct((kinds, block, lanes), BF16 if n else F32) for n in range(count)],
        compiler_params=params(),
        name="add_core",
    )(mine, theirs)


def add_and_pack(mine, theirs, width, after=()):
    kinds, block, lanes = mine.shape
    ratio = lanes // width
    groups = kinds // ratio

    def body(*refs):
        ins, outs = refs[:1 + len(theirs)], refs[1 + len(theirs) + len(after):]
        for g in range(groups):
            sums = []
            for q in range(ratio):
                acc = ins[0][g * ratio + q]
                for ref in ins[1:]:
                    acc = acc + ref[g * ratio + q].astype(F32)
                sums.append(acc)
            for u in range(ratio):
                outs[u][g] = swap_groups(merge(sums, width, u), width, u).astype(BF16)

    return pl.pallas_call(
        body,
        in_specs=[pl.BlockSpec(memory_space=pltpu.VMEM)] * (1 + len(theirs))
        + [pl.BlockSpec(memory_space=pl.ANY)] * len(after),
        out_shape=[jax.ShapeDtypeStruct((groups, block, lanes), BF16)] * ratio,
        compiler_params=params(),
        name="add_and_pack",
    )(mine, *theirs, *after)


def add_core_near(mine, theirs, width, after=()):
    count, kinds, block, lanes = mine.shape
    ratio = lanes // width
    groups = kinds // ratio

    def body(a_ref, b_ref, *refs):
        outs = refs[len(after):]
        for n in range(count):
            for g in range(groups):
                at = n * groups + g
                sums = [
                    a_ref[n, g * ratio + q] + b_ref[n, g * ratio + q].astype(F32) for q in range(ratio)
                ]
                for u in range(ratio):
                    outs[u][at] = swap_groups(merge(sums, width, u), width, u).astype(outs[u].dtype)

    return pl.pallas_call(
        body,
        in_specs=[pl.BlockSpec(memory_space=pltpu.VMEM)] * 2 + [pl.BlockSpec(memory_space=pl.ANY)] * len(after),
        out_shape=[
            jax.ShapeDtypeStruct((count * groups, block, lanes), BF16 if u else F32) for u in range(ratio)
        ],
        compiler_params=params(),
        name="add_core_near",
    )(mine, theirs, *after)


def add_near(mine, theirs, groups, after=()):
    total, block, lanes = mine.shape
    count = total // groups

    def body(*refs):
        ins, outs = refs[:1 + len(theirs)], refs[1 + len(theirs) + len(after):]
        for n in range(count):
            here = slice(n * groups, (n + 1) * groups)
            acc = ins[0][here]
            for ref in ins[1:]:
                acc = acc + ref[here].astype(F32)
            outs[n][...] = acc.astype(outs[n].dtype)

    return pl.pallas_call(
        body,
        in_specs=[pl.BlockSpec(memory_space=pltpu.VMEM)] * (1 + len(theirs))
        + [pl.BlockSpec(memory_space=pl.ANY)] * len(after),
        out_shape=[jax.ShapeDtypeStruct((groups, block, lanes), BF16 if n else F32) for n in range(count)],
        compiler_params=params(),
        name="add_near",
    )(mine, *theirs, *after)


def fold(parts):
    def body(*refs):
        acc = refs[0][...].astype(F32)
        for ref in refs[1:-1]:
            acc = acc + ref[...].astype(F32)
        refs[-1][...] = acc

    return pl.pallas_call(
        body,
        out_shape=jax.ShapeDtypeStruct(parts[0].shape, F32),
        compiler_params=params(),
        name="fold",
    )(*parts)


def finish(parts, kinds, width, scale):
    groups, block, lanes = parts[0].shape
    ratio = lanes // width

    def body(*refs):
        out = refs[-1]
        for g in range(groups):
            acc = refs[0][g]
            for ref in refs[1:-1]:
                acc = acc + ref[g].astype(F32)
            acc = acc * scale
            for q in range(ratio):
                moved = pltpu.roll(acc, lanes - q * width, 1) if q else acc
                out[g * ratio + q] = moved[:, :width]

    return pl.pallas_call(
        body,
        out_shape=jax.ShapeDtypeStruct((kinds, block, width), F32),
        compiler_params=params(),
        name="finish",
    )(*parts)


def volume_grad(deltas, weights, shape):
    cells_x, cells_y, cells_z, in_chan = shape
    nx, ny, nz = cells_x // 2, cells_y // 2, cells_z // 2
    ratio, rows, out_chan = deltas.shape
    planes = cells_x * cells_y

    def body(d_ref, w_ref, o_hbm, mark_ref, wide_ref, plane_ref, sem):
        mark_ref[...] = jnp.zeros_like(mark_ref)
        row = lax.broadcasted_iota(jnp.int32, (cells_z, nz), 0)
        col = lax.broadcasted_iota(jnp.int32, (cells_z, nz), 1)
        places = sorted({(k % 2, k % ratio) for k in range(8)})
        for n, (e, q) in enumerate(places):
            put = (row == 2 * col + e).astype(F32).astype(BF16)
            for m in range(nx * ny):
                got = jnp.dot(put, d_ref[q, m * nz:(m + 1) * nz], preferred_element_type=F32)
                wide_ref[n, m * cells_z:(m + 1) * cells_z] = got.astype(BF16)
        moves = []
        for a in range(2):
            for b in range(2):
                acc = None
                for e in range(2):
                    k = 4 * a + 2 * b + e
                    part = lax.dot_general(
                        wide_ref[places.index((e, k % ratio))], w_ref[k], (((1,), (1,)), ((), ())),
                        preferred_element_type=F32,
                    )
                    acc = part if acc is None else acc + part
                out = acc.astype(BF16)
                for m in range(nx * ny):
                    x, y = 2 * (m // ny) + a, 2 * (m % ny) + b
                    at = len(moves)
                    plane_ref[at] = out[m * cells_z:(m + 1) * cells_z]
                    move = pltpu.make_async_copy(plane_ref.at[at], o_hbm.at[x, y], sem.at[at])
                    move.start()
                    moves.append(move)
        for move in moves:
            move.wait()

    return pl.pallas_call(
        body,
        in_specs=[pl.BlockSpec(memory_space=pltpu.VMEM)] * 2,
        out_specs=[pl.BlockSpec(memory_space=pl.ANY), pl.BlockSpec(memory_space=pltpu.VMEM)],
        out_shape=[jax.ShapeDtypeStruct(shape, BF16), jax.ShapeDtypeStruct((8, LANES), F32)],
        scratch_shapes=[
            pltpu.VMEM((max(2, ratio), 4 * rows // 2, out_chan), BF16),
            pltpu.VMEM((planes, cells_z, in_chan), BF16),
            pltpu.SemaphoreType.DMA((planes,)),
        ],
        compiler_params=params(),
        cost_estimate=cost(32 * rows * in_chan * out_chan, 2 * rows * 8 * in_chan),
        name="volume_grad",
    )(deltas, weights)


def shards(spaces, chans, volume, weight, cotangent):
    kinds, block, width = weight.shape
    ratio = max(1, LANES // width)
    out_rows = volume.shape[0] * volume.shape[1] * volume.shape[2] // 8

    def pairs(count, step):
        return [(d, other(d, step)) for d in range(count)]

    packed = pack_weight(weight, ratio)
    line = [packed[0]] + [fetch(packed[i % ratio], "chan", pairs(chans, i)) for i in range(1, chans)]
    lane_tiles = chans // ratio
    own = [merge_tile(line[t * ratio:(t + 1) * ratio], width) for t in range(lane_tiles)]
    tiles = pack_cot(cotangent.transpose(0, 1, 3, 2), chans, own[:1])
    cots = [tiles[0]] + [fetch(tiles[i], "chan", pairs(chans, i)) for i in range(1, chans)]
    upstream = turn_cot(cots)
    patches, turned = patch_rows(volume, own[1:])
    lines = []
    for j in range(0, spaces, 2):
        lines.append([fetch(tile, "space", pairs(spaces, j)) for tile in own] if j else own)
        lines.append([fetch(gate(tile, (patches,)) if not j and not t else gate(tile, (patches,)) if not j else gate(tile, (upstream,)) if not t else gate(tile, (upstream,)), "space", pairs(spaces, 1)) for t, tile in enumerate(lines[-1])])
    own_part = None
    if 2 * block % LANES == 0 and spaces > 2:
        own_part = forward_own(patches, lines[:2], spaces, width, ratio)
    deltas, weights = forward(patches, own_part, lines, upstream, width, ratio)
    steps = list(range(0, spaces, 2))
    lanes = ratio * width
    away = weight_part(turned, deltas, [s + 1 for s in steps], spaces, lanes, BF16)
    crossed = [fetch(tile, "space", pairs(spaces, 1)) for tile in away]
    near = weight_part(turned, deltas, steps, spaces, lanes, F32)
    grad_volume, mark = volume_grad(deltas, weights, volume.shape)
    far, outs = [], []
    for t in reversed(range(1, lane_tiles)):
        sums = add_core(near[t], crossed[t])
        far = list(sums[1:]) + far
        came = [fetch(sums[n], "space", pairs(spaces, steps[n])) for n in range(1, len(steps))]
        outs += [(t * ratio + u, part) for u, part in enumerate(add_and_pack(sums[0], came, width, (mark,)))]
    parts = add_core_near(near[0], crossed[0], width, far[:1] + [mark])
    got = [fetch(parts[u], "chan", pairs(chans, u)) for u in range(1, ratio)]
    sums = add_near(parts[0], got, kinds // ratio, [part for _, part in outs[-1:]])
    got = [sums[0]] + [fetch(sums[n], "space", pairs(spaces, steps[n])) for n in range(1, len(steps))]
    spread_out = [fetch(part, "chan", pairs(chans, i)) for i, part in outs]
    got += [fold(spread_out)] if spread_out else []
    grad_weight = finish(got, kinds, width, 1.0 / out_rows)
    return (grad_volume, grad_weight)


def solution(mesh):
    return jax.shard_map(
        functools.partial(shards, mesh.shape["space"], mesh.shape["chan"]),
        mesh=mesh,
        in_specs=(
            P(("groups", "space"), "chan", None, None),
            P(None, "space", "chan"),
            P(("groups", "space"), None, None, "chan"),
        ),
        out_specs=(P(("groups", "space"), "chan", None, None), P("groups", "space", "chan")),
        check_vma=False,
    )
```

```python
import functools

import jax
import jax.numpy as jnp
from jax import lax
from jax.experimental import pallas as pl
from jax.experimental.pallas import tpu as pltpu
from jax.sharding import PartitionSpec as P

LANES = 128
TURN_FLOPS = 4 * 10**9
BF16 = jnp.bfloat16
F32 = jnp.float32


def other(me, step):
    return me ^ step


def fetch(x, axis, pairs):
    return lax.ppermute(x, axis, pairs)


def lane_group(shape, width):
    return lax.broadcasted_iota(jnp.int32, shape, len(shape) - 1) // width


def merge(parts, width, flip):
    group = lane_group(parts[0].shape, width)
    out = parts[flip]
    for g in range(1, len(parts)):
        out = jnp.where(group == g, parts[g ^ flip], out)
    return out


def swap_groups(x, width, flip):
    if flip == 0:
        return x
    tiles = []
    for t in range(x.shape[1] // LANES):
        tile = x[:, t * LANES:(t + 1) * LANES]
        bit = 1
        while bit <= flip:
            if flip & bit:
                shift = width * bit
                up = pltpu.roll(tile, LANES - shift, 1)
                if 2 * shift == LANES:
                    tile = up
                else:
                    even = (lane_group(tile.shape, shift) % 2) == 0
                    tile = jnp.where(even, up, pltpu.roll(tile, shift, 1))
            bit *= 2
        tiles.append(tile)
    return tiles[0] if len(tiles) == 1 else jnp.concatenate(tiles, axis=1)


def whole(x):
    return pl.BlockSpec(x.shape, lambda *_: (0,) * len(x.shape))


def params():
    return pltpu.CompilerParams(vmem_limit_bytes=48 * 1024 * 1024)


def cost(flops, bytes_accessed):
    return pl.CostEstimate(flops=flops, bytes_accessed=bytes_accessed, transcendentals=0)


def spread(x, width, at):
    if width >= LANES:
        return x
    zeros = jnp.zeros((x.shape[0], LANES - width), x.dtype)
    full = jnp.concatenate([x, zeros], axis=1)
    return pltpu.roll(full, at * width, 1) if at else full


def pack_weight(weight, ratio):
    kinds, rows, width = weight.shape
    groups = kinds // ratio
    lanes = ratio * width

    def body(w_ref, *outs):
        for g in range(groups):
            for flip in range(ratio):
                acc = None
                for lane in range(ratio):
                    part = spread(w_ref[g * ratio + (lane ^ flip)].astype(F32), width, lane)
                    acc = part if acc is None else acc + part
                outs[flip][g] = acc.astype(BF16)

    return pl.pallas_call(
        body,
        out_shape=[jax.ShapeDtypeStruct((groups, rows, lanes), BF16)] * ratio,
        compiler_params=params(),
        name="pack_weight",
    )(weight)


def pack_cot(cot, chans, after=()):
    planes, cells_y, width, cells_z = cot.shape
    own_y = cells_y // chans

    def body(c_ref, *refs):
        outs = refs[len(after):]
        me = lax.axis_index("chan")
        for step in range(chans):
            target = other(me, step) * own_y
            for p in range(planes):
                for y in range(own_y):
                    outs[step][p * own_y + y] = c_ref[p, target + y]

    return pl.pallas_call(
        body,
        in_specs=[pl.BlockSpec(memory_space=pltpu.VMEM)] + [pl.BlockSpec(memory_space=pl.ANY)] * len(after),
        out_shape=[jax.ShapeDtypeStruct((planes * own_y, width, cells_z), BF16)] * chans,
        compiler_params=params(),
        name="pack_cot",
    )(cot, *after)


def merge_tile(parts, width, after=()):
    groups, block, lanes = parts[0].shape
    ratio = len(parts)

    def body(*refs):
        out = refs[-1]
        for g in range(groups):
            got = [refs[u][g] for u in range(ratio)]
            for q in range(ratio):
                out[g * ratio + q] = merge(got, width, q)

    return pl.pallas_call(
        body,
        in_specs=[pl.BlockSpec(memory_space=pltpu.VMEM)] * ratio + [pl.BlockSpec(memory_space=pl.ANY)] * len(after),
        out_shape=jax.ShapeDtypeStruct((groups * ratio, block, lanes), BF16),
        compiler_params=params(),
        name="merge_tile",
    )(*parts, *after)


def gate(tile, after):
    def body(t_ref, *refs):
        refs[-1][...] = t_ref[...]

    return pl.pallas_call(
        body,
        in_specs=[pl.BlockSpec(memory_space=pltpu.VMEM)] + [pl.BlockSpec(memory_space=pl.ANY)] * len(after),
        out_shape=jax.ShapeDtypeStruct(tile.shape, tile.dtype),
        compiler_params=params(),
        name="gate",
    )(tile, *after)


def patch_rows(volume, after=()):
    cells_x, cells_y, cells_z, in_chan = volume.shape
    nx, ny, nz = cells_x // 2, cells_y // 2, cells_z // 2
    rows = nx * ny * nz

    def body(v_ref, *refs):
        p_ref, t_ref = refs[-2:]
        row = lax.broadcasted_iota(jnp.int32, (cells_z, cells_z), 0)
        col = lax.broadcasted_iota(jnp.int32, (cells_z, cells_z), 1)
        pick = (col == 2 * (row % nz) + row // nz).astype(F32).astype(BF16)
        for n in range(nx * ny):
            here = slice(n * nz, (n + 1) * nz)
            for a in range(2):
                for b in range(2):
                    k = 4 * a + 2 * b
                    got = jnp.dot(pick, v_ref[2 * (n // ny) + a, 2 * (n % ny) + b], preferred_element_type=F32)
                    got = got.astype(BF16)
                    for e in range(2):
                        part = got[e * nz:(e + 1) * nz]
                        p_ref[k + e, here] = part
                        t_ref[k + e, :, here] = part.T

    return pl.pallas_call(
        body,
        in_specs=[pl.BlockSpec(memory_space=pltpu.VMEM)] + [pl.BlockSpec(memory_space=pl.ANY)] * len(after),
        out_shape=[
            jax.ShapeDtypeStruct((8, rows, in_chan), BF16),
            jax.ShapeDtypeStruct((8, in_chan, rows), BF16),
        ],
        compiler_params=params(),
        cost_estimate=cost(16 * rows * in_chan * cells_z, 6 * volume.size),
        name="patch_rows",
    )(volume, *after)


def turn_cot(cots):
    tiles, width, cells = cots[0].shape
    out_chan = width * len(cots)

    def body(*refs):
        out = refs[-1]
        for n in range(tiles):
            column = jnp.concatenate([ref[n] for ref in refs[:-1]], axis=0)
            out[n * cells:(n + 1) * cells] = column.T

    return pl.pallas_call(
        body,
        out_shape=jax.ShapeDtypeStruct((tiles * cells, out_chan), BF16),
        compiler_params=params(),
        cost_estimate=cost(TURN_FLOPS, 4 * tiles * cells * out_chan),
        name="turn_cot",
    )(*cots)


def place(w_ref, ins, me, first, tiles):
    kinds, block, lanes = ins[0].shape
    for n in range(len(ins) // tiles):
        at = pl.multiple_of(other(me, first + n) * block, block)
        for t in range(tiles):
            for k in range(kinds):
                w_ref[k, pl.ds(at, block), t * lanes:(t + 1) * lanes] = ins[n * tiles + t][k]


def chip_part(p_ref, w_ref, here, me, chip, block, ratio, q):
    kinds = w_ref.shape[0]
    span = 2 * block
    at = pl.multiple_of(other(me, chip) // 2 * span, span)
    ks = range(q, kinds, ratio)
    per = max(1, min(len(ks), w_ref.shape[1] // span))
    acc = None
    for first in range(0, len(ks), per):
        some = ks[first:first + per]
        left = jnp.concatenate([p_ref[k, here, pl.ds(at, span)] for k in some], axis=1)
        right = jnp.concatenate([w_ref[k, pl.ds(at, span)] for k in some], axis=0)
        part = jnp.dot(left, right, preferred_element_type=F32)
        acc = part if acc is None else acc + part
    return acc


def forward_own(patches, lines, spaces, width, ratio):
    kinds, rows, in_chan = patches.shape
    _, block, lanes = lines[0][0].shape
    tiles = len(lines[0])
    out_chan = tiles * lanes
    flat = [tile for line in lines for tile in line]

    def body(p_ref, *refs):
        pre_ref, w_ref = refs[-2:]
        me = lax.axis_index("space")
        place(w_ref, refs[:-2], me, 0, tiles)
        for first in range(0, rows, rows // 2):
            here = slice(first, first + rows // 2)
            pre = None
            for q in range(ratio):
                acc = swap_groups(chip_part(p_ref, w_ref, here, me, 0, block, ratio, q), width, q)
                pre = acc if pre is None else pre + acc
            pre_ref[here] = pre

    return pl.pallas_call(
        body,
        out_shape=[
            jax.ShapeDtypeStruct((rows, out_chan), F32),
            jax.ShapeDtypeStruct((kinds, in_chan, out_chan), BF16),
        ],
        compiler_params=params(),
        cost_estimate=cost(4 * patches.size * out_chan // spaces, 2 * patches.size),
        name="forward_own",
    )(patches, *flat)


def forward(patches, own, lines, upstream, width, ratio):
    kinds, rows, in_chan = patches.shape
    tiles = len(lines[0])
    _, block, lanes = lines[0][0].shape
    out_chan = tiles * lanes
    spaces = len(lines)
    start = 0 if own is None else 2
    flat = [tile for line in lines[start:] for tile in line]

    def body(p_ref, u_ref, *refs):
        d_ref, w_ref = refs[-2:]
        me = lax.axis_index("space")
        place(w_ref, refs[:len(flat)], me, start, tiles)
        for first in range(0, rows, rows // 4):
            here = slice(first, first + rows // 4)
            pre = None if own is None else refs[len(flat)][here]
            for q in range(ratio):
                acc = None
                if own is None:
                    for k in range(q, kinds, ratio):
                        part = jnp.dot(p_ref[k, here], w_ref[k], preferred_element_type=F32)
                        acc = part if acc is None else acc + part
                else:
                    for chip in range(start, spaces, 2):
                        part = chip_part(p_ref, w_ref, here, me, chip, block, ratio, q)
                        acc = part if acc is None else acc + part
                acc = swap_groups(acc, width, q)
                pre = acc if pre is None else pre + acc
            up = u_ref[here].astype(F32)
            squash = 0.5 + 0.5 * jnp.tanh(0.5 * pre)
            slopes = squash * (1.0 + pre * (1.0 - squash))
            delta = (up * slopes).astype(BF16)
            d_ref[0, here] = delta
            for q in range(1, ratio):
                d_ref[q, here] = swap_groups(delta.astype(F32), width, q).astype(BF16)

    extra = () if own is None else own
    return pl.pallas_call(
        body,
        out_shape=[
            jax.ShapeDtypeStruct((ratio, rows, out_chan), BF16),
            jax.ShapeDtypeStruct((kinds, in_chan, out_chan), BF16),
        ],
        input_output_aliases={} if own is None else {2 + len(flat) + 1: 1},
        compiler_params=params(),
        cost_estimate=cost(2 * patches.size * out_chan, 2 * patches.size),
        name="forward",
    )(patches, upstream, *flat, *extra)


def weight_part(turned, deltas, steps, spaces, lanes, dtype):
    kinds, in_chan, rows = turned.shape
    ratio, _, out_chan = deltas.shape
    block = in_chan // spaces
    tiles = out_chan // lanes

    def body(t_ref, d_ref, *outs):
        me = lax.axis_index("space")
        ats = [pl.multiple_of(other(me, step) * block, block) for step in steps]
        for q in range(ratio):
            ks = range(q, kinds, ratio)
            for n, at in enumerate(ats):
                left = jnp.concatenate([t_ref[k, pl.ds(at, block)] for k in ks], axis=0)
                got = jnp.dot(left, d_ref[q], preferred_element_type=F32).astype(dtype)
                for i, k in enumerate(ks):
                    for t in range(tiles):
                        outs[t][n, k] = got[i * block:(i + 1) * block, t * lanes:(t + 1) * lanes]

    return pl.pallas_call(
        body,
        out_shape=[jax.ShapeDtypeStruct((len(steps), kinds, block, lanes), dtype)] * tiles,
        compiler_params=params(),
        cost_estimate=cost(2 * turned.size * out_chan * len(steps) // spaces, 2 * turned.size),
        name="weight_part",
    )(turned, deltas)


def add_core(mine, theirs):
    count, kinds, block, lanes = mine.shape

    def body(a_ref, b_ref, *outs):
        for n in range(count):
            outs[n][...] = (a_ref[n] + b_ref[n].astype(F32)).astype(outs[n].dtype)

    return pl.pallas_call(
        body,
        out_shape=[jax.ShapeDtypeStruct((kinds, block, lanes), BF16 if n else F32) for n in range(count)],
        compiler_params=params(),
        name="add_core",
    )(mine, theirs)


def add_and_pack(mine, theirs, width, after=()):
    kinds, block, lanes = mine.shape
    ratio = lanes // width
    groups = kinds // ratio

    def body(*refs):
        ins, outs = refs[:1 + len(theirs)], refs[1 + len(theirs) + len(after):]
        for g in range(groups):
            sums = []
            for q in range(ratio):
                acc = ins[0][g * ratio + q]
                for ref in ins[1:]:
                    acc = acc + ref[g * ratio + q].astype(F32)
                sums.append(acc)
            for u in range(ratio):
                outs[u][g] = swap_groups(merge(sums, width, u), width, u).astype(BF16)

    return pl.pallas_call(
        body,
        in_specs=[pl.BlockSpec(memory_space=pltpu.VMEM)] * (1 + len(theirs))
        + [pl.BlockSpec(memory_space=pl.ANY)] * len(after),
        out_shape=[jax.ShapeDtypeStruct((groups, block, lanes), BF16)] * ratio,
        compiler_params=params(),
        name="add_and_pack",
    )(mine, *theirs, *after)


def add_core_near(mine, theirs, width, after=()):
    count, kinds, block, lanes = mine.shape
    ratio = lanes // width
    groups = kinds // ratio

    def body(a_ref, b_ref, *refs):
        outs = refs[len(after):]
        for n in range(count):
            for g in range(groups):
                at = n * groups + g
                sums = [
                    a_ref[n, g * ratio + q] + b_ref[n, g * ratio + q].astype(F32) for q in range(ratio)
                ]
                for u in range(ratio):
                    outs[u][at] = swap_groups(merge(sums, width, u), width, u).astype(outs[u].dtype)

    return pl.pallas_call(
        body,
        in_specs=[pl.BlockSpec(memory_space=pltpu.VMEM)] * 2 + [pl.BlockSpec(memory_space=pl.ANY)] * len(after),
        out_shape=[
            jax.ShapeDtypeStruct((count * groups, block, lanes), BF16 if u else F32) for u in range(ratio)
        ],
        compiler_params=params(),
        name="add_core_near",
    )(mine, theirs, *after)


def add_near(mine, theirs, groups, after=()):
    total, block, lanes = mine.shape
    count = total // groups

    def body(*refs):
        ins, outs = refs[:1 + len(theirs)], refs[1 + len(theirs) + len(after):]
        for n in range(count):
            here = slice(n * groups, (n + 1) * groups)
            acc = ins[0][here]
            for ref in ins[1:]:
                acc = acc + ref[here].astype(F32)
            outs[n][...] = acc.astype(outs[n].dtype)

    return pl.pallas_call(
        body,
        in_specs=[pl.BlockSpec(memory_space=pltpu.VMEM)] * (1 + len(theirs))
        + [pl.BlockSpec(memory_space=pl.ANY)] * len(after),
        out_shape=[jax.ShapeDtypeStruct((groups, block, lanes), BF16 if n else F32) for n in range(count)],
        compiler_params=params(),
        name="add_near",
    )(mine, *theirs, *after)


def fold(parts):
    def body(*refs):
        acc = refs[0][...].astype(F32)
        for ref in refs[1:-1]:
            acc = acc + ref[...].astype(F32)
        refs[-1][...] = acc

    return pl.pallas_call(
        body,
        out_shape=jax.ShapeDtypeStruct(parts[0].shape, F32),
        compiler_params=params(),
        name="fold",
    )(*parts)


def finish(parts, kinds, width, scale):
    groups, block, lanes = parts[0].shape
    ratio = lanes // width

    def body(*refs):
        out = refs[-1]
        for g in range(groups):
            acc = refs[0][g]
            for ref in refs[1:-1]:
                acc = acc + ref[g].astype(F32)
            acc = acc * scale
            for q in range(ratio):
                moved = pltpu.roll(acc, lanes - q * width, 1) if q else acc
                out[g * ratio + q] = moved[:, :width]

    return pl.pallas_call(
        body,
        out_shape=jax.ShapeDtypeStruct((kinds, block, width), F32),
        compiler_params=params(),
        name="finish",
    )(*parts)


def volume_grad(deltas, weights, shape):
    cells_x, cells_y, cells_z, in_chan = shape
    nx, ny, nz = cells_x // 2, cells_y // 2, cells_z // 2
    ratio, rows, out_chan = deltas.shape
    planes = cells_x * cells_y

    def body(d_ref, w_ref, o_hbm, mark_ref, wide_ref, plane_ref, sem):
        mark_ref[...] = jnp.zeros_like(mark_ref)
        row = lax.broadcasted_iota(jnp.int32, (cells_z, nz), 0)
        col = lax.broadcasted_iota(jnp.int32, (cells_z, nz), 1)
        places = sorted({(k % 2, k % ratio) for k in range(8)})
        for n, (e, q) in enumerate(places):
            put = (row == 2 * col + e).astype(F32).astype(BF16)
            for m in range(nx * ny):
                got = jnp.dot(put, d_ref[q, m * nz:(m + 1) * nz], preferred_element_type=F32)
                wide_ref[n, m * cells_z:(m + 1) * cells_z] = got.astype(BF16)
        moves = []
        for a in range(2):
            for b in range(2):
                acc = None
                for e in range(2):
                    k = 4 * a + 2 * b + e
                    part = lax.dot_general(
                        wide_ref[places.index((e, k % ratio))], w_ref[k], (((1,), (1,)), ((), ())),
                        preferred_element_type=F32,
                    )
                    acc = part if acc is None else acc + part
                out = acc.astype(BF16)
                for m in range(nx * ny):
                    x, y = 2 * (m // ny) + a, 2 * (m % ny) + b
                    at = len(moves)
                    plane_ref[at] = out[m * cells_z:(m + 1) * cells_z]
                    move = pltpu.make_async_copy(plane_ref.at[at], o_hbm.at[x, y], sem.at[at])
                    move.start()
                    moves.append(move)
        for move in moves:
            move.wait()

    return pl.pallas_call(
        body,
        in_specs=[pl.BlockSpec(memory_space=pltpu.VMEM)] * 2,
        out_specs=[pl.BlockSpec(memory_space=pl.ANY), pl.BlockSpec(memory_space=pltpu.VMEM)],
        out_shape=[jax.ShapeDtypeStruct(shape, BF16), jax.ShapeDtypeStruct((8, LANES), F32)],
        scratch_shapes=[
            pltpu.VMEM((max(2, ratio), 4 * rows // 2, out_chan), BF16),
            pltpu.VMEM((planes, cells_z, in_chan), BF16),
            pltpu.SemaphoreType.DMA((planes,)),
        ],
        compiler_params=params(),
        cost_estimate=cost(32 * rows * in_chan * out_chan, 2 * rows * 8 * in_chan),
        name="volume_grad",
    )(deltas, weights)


def shards(spaces, chans, volume, weight, cotangent):
    kinds, block, width = weight.shape
    ratio = max(1, LANES // width)
    out_rows = volume.shape[0] * volume.shape[1] * volume.shape[2] // 8

    def pairs(count, step):
        return [(d, other(d, step)) for d in range(count)]

    packed = pack_weight(weight, ratio)
    line = [packed[0]] + [fetch(packed[i % ratio], "chan", pairs(chans, i)) for i in range(1, chans)]
    lane_tiles = chans // ratio
    own = [merge_tile(line[t * ratio:(t + 1) * ratio], width) for t in range(lane_tiles)]
    tiles = pack_cot(cotangent.transpose(0, 1, 3, 2), chans, own[:1])
    cots = [tiles[0]] + [fetch(tiles[i], "chan", pairs(chans, i)) for i in range(1, chans)]
    upstream = turn_cot(cots)
    patches, turned = patch_rows(volume, own[1:])
    lines = []
    for j in range(0, spaces, 2):
        lines.append([fetch(tile, "space", pairs(spaces, j)) for tile in own] if j else own)
        lines.append([fetch(gate(tile, (patches,)) if not j and not t else gate(tile, (patches,)) if not j else gate(tile, (upstream,)) if not t else gate(tile, (upstream,)), "space", pairs(spaces, 1)) for t, tile in enumerate(lines[-1])])
    own_part = None
    if 2 * block % LANES == 0 and spaces > 2:
        own_part = forward_own(patches, lines[:2], spaces, width, ratio)
    deltas, weights = forward(patches, own_part, lines, upstream, width, ratio)
    steps = list(range(0, spaces, 2))
    lanes = ratio * width
    away = weight_part(turned, deltas, [s + 1 for s in steps], spaces, lanes, BF16)
    crossed = [fetch(tile, "space", pairs(spaces, 1)) for tile in away]
    near = weight_part(turned, deltas, steps, spaces, lanes, F32)
    grad_volume, mark = volume_grad(deltas, weights, volume.shape)
    far, outs = [], []
    for t in reversed(range(1, lane_tiles)):
        sums = add_core(near[t], crossed[t])
        far = list(sums[1:]) + far
        came = [fetch(sums[n], "space", pairs(spaces, steps[n])) for n in range(1, len(steps))]
        outs += [(t * ratio + u, part) for u, part in enumerate(add_and_pack(sums[0], came, width, (mark,)))]
    parts = add_core_near(near[0], crossed[0], width, far[:1] + [mark])
    got = [fetch(parts[u], "chan", pairs(chans, u)) for u in range(1, ratio)]
    sums = add_near(parts[0], got, kinds // ratio, [part for _, part in outs[-1:]])
    got = [sums[0]] + [fetch(sums[n], "space", pairs(spaces, steps[n])) for n in range(1, len(steps))]
    spread_out = [fetch(part, "chan", pairs(chans, i)) for i, part in outs]
    got += [fold(spread_out)] if spread_out else []
    grad_weight = finish(got, kinds, width, 1.0 / out_rows)
    return (grad_volume, grad_weight)


def solution(mesh):
    return jax.shard_map(
        functools.partial(shards, mesh.shape["space"], mesh.shape["chan"]),
        mesh=mesh,
        in_specs=(
            P(("groups", "space"), "chan", None, None),
            P(None, "space", "chan"),
            P(("groups", "space"), None, None, "chan"),
        ),
        out_specs=(P(("groups", "space"), "chan", None, None), P("groups", "space", "chan")),
        check_vma=False,
    )
```

```python
import functools

import jax
import jax.numpy as jnp
from jax import lax
from jax.experimental import pallas as pl
from jax.experimental.pallas import tpu as pltpu
from jax.sharding import PartitionSpec as P

LANES = 128
TURN_FLOPS = 4 * 10**9
BF16 = jnp.bfloat16
F32 = jnp.float32


def other(me, step):
    return me ^ step


def fetch(x, axis, pairs):
    return lax.ppermute(x, axis, pairs)


def lane_group(shape, width):
    return lax.broadcasted_iota(jnp.int32, shape, len(shape) - 1) // width


def merge(parts, width, flip):
    group = lane_group(parts[0].shape, width)
    out = parts[flip]
    for g in range(1, len(parts)):
        out = jnp.where(group == g, parts[g ^ flip], out)
    return out


def swap_groups(x, width, flip):
    if flip == 0:
        return x
    tiles = []
    for t in range(x.shape[1] // LANES):
        tile = x[:, t * LANES:(t + 1) * LANES]
        bit = 1
        while bit <= flip:
            if flip & bit:
                shift = width * bit
                up = pltpu.roll(tile, LANES - shift, 1)
                if 2 * shift == LANES:
                    tile = up
                else:
                    even = (lane_group(tile.shape, shift) % 2) == 0
                    tile = jnp.where(even, up, pltpu.roll(tile, shift, 1))
            bit *= 2
        tiles.append(tile)
    return tiles[0] if len(tiles) == 1 else jnp.concatenate(tiles, axis=1)


def whole(x):
    return pl.BlockSpec(x.shape, lambda *_: (0,) * len(x.shape))


def params():
    return pltpu.CompilerParams(vmem_limit_bytes=48 * 1024 * 1024)


def cost(flops, bytes_accessed):
    return pl.CostEstimate(flops=flops, bytes_accessed=bytes_accessed, transcendentals=0)


def spread(x, width, at):
    if width >= LANES:
        return x
    zeros = jnp.zeros((x.shape[0], LANES - width), x.dtype)
    full = jnp.concatenate([x, zeros], axis=1)
    return pltpu.roll(full, at * width, 1) if at else full


def pack_weight(weight, ratio):
    kinds, rows, width = weight.shape
    groups = kinds // ratio
    lanes = ratio * width

    def body(w_ref, *outs):
        for g in range(groups):
            for flip in range(ratio):
                acc = None
                for lane in range(ratio):
                    part = spread(w_ref[g * ratio + (lane ^ flip)].astype(F32), width, lane)
                    acc = part if acc is None else acc + part
                outs[flip][g] = acc.astype(BF16)

    return pl.pallas_call(
        body,
        out_shape=[jax.ShapeDtypeStruct((groups, rows, lanes), BF16)] * ratio,
        compiler_params=params(),
        name="pack_weight",
    )(weight)


def pack_cot(cot, chans, after=()):
    planes, cells_y, width, cells_z = cot.shape
    own_y = cells_y // chans

    def body(c_ref, *refs):
        outs = refs[len(after):]
        me = lax.axis_index("chan")
        for step in range(chans):
            target = other(me, step) * own_y
            for p in range(planes):
                for y in range(own_y):
                    outs[step][p * own_y + y] = c_ref[p, target + y]

    return pl.pallas_call(
        body,
        in_specs=[pl.BlockSpec(memory_space=pltpu.VMEM)] + [pl.BlockSpec(memory_space=pl.ANY)] * len(after),
        out_shape=[jax.ShapeDtypeStruct((planes * own_y, width, cells_z), BF16)] * chans,
        compiler_params=params(),
        name="pack_cot",
    )(cot, *after)


def merge_tile(parts, width, after=()):
    groups, block, lanes = parts[0].shape
    ratio = len(parts)

    def body(*refs):
        out = refs[-1]
        for g in range(groups):
            got = [refs[u][g] for u in range(ratio)]
            for q in range(ratio):
                out[g * ratio + q] = merge(got, width, q)

    return pl.pallas_call(
        body,
        in_specs=[pl.BlockSpec(memory_space=pltpu.VMEM)] * ratio + [pl.BlockSpec(memory_space=pl.ANY)] * len(after),
        out_shape=jax.ShapeDtypeStruct((groups * ratio, block, lanes), BF16),
        compiler_params=params(),
        name="merge_tile",
    )(*parts, *after)


def gate(tile, after):
    def body(t_ref, *refs):
        refs[-1][...] = t_ref[...]

    return pl.pallas_call(
        body,
        in_specs=[pl.BlockSpec(memory_space=pltpu.VMEM)] + [pl.BlockSpec(memory_space=pl.ANY)] * len(after),
        out_shape=jax.ShapeDtypeStruct(tile.shape, tile.dtype),
        compiler_params=params(),
        name="gate",
    )(tile, *after)


def patch_rows(volume, after=()):
    cells_x, cells_y, cells_z, in_chan = volume.shape
    nx, ny, nz = cells_x // 2, cells_y // 2, cells_z // 2
    rows = nx * ny * nz

    def body(v_ref, *refs):
        p_ref, t_ref = refs[-2:]
        row = lax.broadcasted_iota(jnp.int32, (cells_z, cells_z), 0)
        col = lax.broadcasted_iota(jnp.int32, (cells_z, cells_z), 1)
        pick = (col == 2 * (row % nz) + row // nz).astype(F32).astype(BF16)
        for n in range(nx * ny):
            here = slice(n * nz, (n + 1) * nz)
            for a in range(2):
                for b in range(2):
                    k = 4 * a + 2 * b
                    got = jnp.dot(pick, v_ref[2 * (n // ny) + a, 2 * (n % ny) + b], preferred_element_type=F32)
                    got = got.astype(BF16)
                    for e in range(2):
                        part = got[e * nz:(e + 1) * nz]
                        p_ref[k + e, here] = part
                        t_ref[k + e, :, here] = part.T

    return pl.pallas_call(
        body,
        in_specs=[pl.BlockSpec(memory_space=pltpu.VMEM)] + [pl.BlockSpec(memory_space=pl.ANY)] * len(after),
        out_shape=[
            jax.ShapeDtypeStruct((8, rows, in_chan), BF16),
            jax.ShapeDtypeStruct((8, in_chan, rows), BF16),
        ],
        compiler_params=params(),
        cost_estimate=cost(16 * rows * in_chan * cells_z, 6 * volume.size),
        name="patch_rows",
    )(volume, *after)


def turn_cot(cots):
    tiles, width, cells = cots[0].shape
    out_chan = width * len(cots)

    def body(*refs):
        out = refs[-1]
        for n in range(tiles):
            column = jnp.concatenate([ref[n] for ref in refs[:-1]], axis=0)
            out[n * cells:(n + 1) * cells] = column.T

    return pl.pallas_call(
        body,
        out_shape=jax.ShapeDtypeStruct((tiles * cells, out_chan), BF16),
        compiler_params=params(),
        cost_estimate=cost(TURN_FLOPS, 4 * tiles * cells * out_chan),
        name="turn_cot",
    )(*cots)


def place(w_ref, ins, me, first, tiles):
    kinds, block, lanes = ins[0].shape
    for n in range(len(ins) // tiles):
        at = pl.multiple_of(other(me, first + n) * block, block)
        for t in range(tiles):
            for k in range(kinds):
                w_ref[k, pl.ds(at, block), t * lanes:(t + 1) * lanes] = ins[n * tiles + t][k]


def chip_part(p_ref, w_ref, here, me, chip, block, ratio, q):
    kinds = w_ref.shape[0]
    span = 2 * block
    at = pl.multiple_of(other(me, chip) // 2 * span, span)
    ks = range(q, kinds, ratio)
    per = max(1, min(len(ks), w_ref.shape[1] // span))
    acc = None
    for first in range(0, len(ks), per):
        some = ks[first:first + per]
        left = jnp.concatenate([p_ref[k, here, pl.ds(at, span)] for k in some], axis=1)
        right = jnp.concatenate([w_ref[k, pl.ds(at, span)] for k in some], axis=0)
        part = jnp.dot(left, right, preferred_element_type=F32)
        acc = part if acc is None else acc + part
    return acc


def forward_own(patches, lines, spaces, width, ratio):
    kinds, rows, in_chan = patches.shape
    _, block, lanes = lines[0][0].shape
    tiles = len(lines[0])
    out_chan = tiles * lanes
    flat = [tile for line in lines for tile in line]

    def body(p_ref, *refs):
        pre_ref, w_ref = refs[-2:]
        me = lax.axis_index("space")
        place(w_ref, refs[:-2], me, 0, tiles)
        for first in range(0, rows, rows // 4):
            here = slice(first, first + rows // 4)
            pre = None
            for q in range(ratio):
                acc = swap_groups(chip_part(p_ref, w_ref, here, me, 0, block, ratio, q), width, q)
                pre = acc if pre is None else pre + acc
            pre_ref[here] = pre

    return pl.pallas_call(
        body,
        out_shape=[
            jax.ShapeDtypeStruct((rows, out_chan), F32),
            jax.ShapeDtypeStruct((kinds, in_chan, out_chan), BF16),
        ],
        compiler_params=params(),
        cost_estimate=cost(4 * patches.size * out_chan // spaces, 2 * patches.size),
        name="forward_own",
    )(patches, *flat)


def forward(patches, own, lines, upstream, width, ratio):
    kinds, rows, in_chan = patches.shape
    tiles = len(lines[0])
    _, block, lanes = lines[0][0].shape
    out_chan = tiles * lanes
    spaces = len(lines)
    start = 0 if own is None else 2
    flat = [tile for line in lines[start:] for tile in line]

    def body(p_ref, u_ref, *refs):
        d_ref, w_ref = refs[-2:]
        me = lax.axis_index("space")
        place(w_ref, refs[:len(flat)], me, start, tiles)
        for first in range(0, rows, rows // 4):
            here = slice(first, first + rows // 4)
            pre = None if own is None else refs[len(flat)][here]
            for q in range(ratio):
                acc = None
                if own is None:
                    for k in range(q, kinds, ratio):
                        part = jnp.dot(p_ref[k, here], w_ref[k], preferred_element_type=F32)
                        acc = part if acc is None else acc + part
                else:
                    for chip in range(start, spaces, 2):
                        part = chip_part(p_ref, w_ref, here, me, chip, block, ratio, q)
                        acc = part if acc is None else acc + part
                acc = swap_groups(acc, width, q)
                pre = acc if pre is None else pre + acc
            up = u_ref[here].astype(F32)
            squash = 1.0 / (1.0 + jnp.exp(-pre))
            slopes = squash * (1.0 + pre * (1.0 - squash))
            delta = (up * slopes).astype(BF16)
            d_ref[0, here] = delta
            for q in range(1, ratio):
                d_ref[q, here] = swap_groups(delta.astype(F32), width, q).astype(BF16)

    extra = () if own is None else own
    return pl.pallas_call(
        body,
        out_shape=[
            jax.ShapeDtypeStruct((ratio, rows, out_chan), BF16),
            jax.ShapeDtypeStruct((kinds, in_chan, out_chan), BF16),
        ],
        input_output_aliases={} if own is None else {2 + len(flat) + 1: 1},
        compiler_params=params(),
        cost_estimate=cost(2 * patches.size * out_chan, 2 * patches.size),
        name="forward",
    )(patches, upstream, *flat, *extra)


def weight_part(turned, deltas, steps, spaces, lanes, dtype):
    kinds, in_chan, rows = turned.shape
    ratio, _, out_chan = deltas.shape
    block = in_chan // spaces
    tiles = out_chan // lanes

    def body(t_ref, d_ref, *outs):
        me = lax.axis_index("space")
        ats = [pl.multiple_of(other(me, step) * block, block) for step in steps]
        for q in range(ratio):
            ks = range(q, kinds, ratio)
            for n, at in enumerate(ats):
                left = jnp.concatenate([t_ref[k, pl.ds(at, block)] for k in ks], axis=0)
                got = jnp.dot(left, d_ref[q], preferred_element_type=F32).astype(dtype)
                for i, k in enumerate(ks):
                    for t in range(tiles):
                        outs[t][n, k] = got[i * block:(i + 1) * block, t * lanes:(t + 1) * lanes]

    return pl.pallas_call(
        body,
        out_shape=[jax.ShapeDtypeStruct((len(steps), kinds, block, lanes), dtype)] * tiles,
        compiler_params=params(),
        cost_estimate=cost(2 * turned.size * out_chan * len(steps) // spaces, 2 * turned.size),
        name="weight_part",
    )(turned, deltas)


def add_core(mine, theirs):
    count, kinds, block, lanes = mine.shape

    def body(a_ref, b_ref, *outs):
        for n in range(count):
            outs[n][...] = (a_ref[n] + b_ref[n].astype(F32)).astype(outs[n].dtype)

    return pl.pallas_call(
        body,
        out_shape=[jax.ShapeDtypeStruct((kinds, block, lanes), BF16 if n else F32) for n in range(count)],
        compiler_params=params(),
        name="add_core",
    )(mine, theirs)


def add_and_pack(mine, theirs, width, after=()):
    kinds, block, lanes = mine.shape
    ratio = lanes // width
    groups = kinds // ratio

    def body(*refs):
        ins, outs = refs[:1 + len(theirs)], refs[1 + len(theirs) + len(after):]
        for g in range(groups):
            sums = []
            for q in range(ratio):
                acc = ins[0][g * ratio + q]
                for ref in ins[1:]:
                    acc = acc + ref[g * ratio + q].astype(F32)
                sums.append(acc)
            for u in range(ratio):
                outs[u][g] = swap_groups(merge(sums, width, u), width, u).astype(BF16)

    return pl.pallas_call(
        body,
        in_specs=[pl.BlockSpec(memory_space=pltpu.VMEM)] * (1 + len(theirs))
        + [pl.BlockSpec(memory_space=pl.ANY)] * len(after),
        out_shape=[jax.ShapeDtypeStruct((groups, block, lanes), BF16)] * ratio,
        compiler_params=params(),
        name="add_and_pack",
    )(mine, *theirs, *after)


def add_core_near(mine, theirs, width, after=()):
    count, kinds, block, lanes = mine.shape
    ratio = lanes // width
    groups = kinds // ratio

    def body(a_ref, b_ref, *refs):
        outs = refs[len(after):]
        for n in range(count):
            for g in range(groups):
                at = n * groups + g
                sums = [
                    a_ref[n, g * ratio + q] + b_ref[n, g * ratio + q].astype(F32) for q in range(ratio)
                ]
                for u in range(ratio):
                    outs[u][at] = swap_groups(merge(sums, width, u), width, u).astype(outs[u].dtype)

    return pl.pallas_call(
        body,
        in_specs=[pl.BlockSpec(memory_space=pltpu.VMEM)] * 2 + [pl.BlockSpec(memory_space=pl.ANY)] * len(after),
        out_shape=[
            jax.ShapeDtypeStruct((count * groups, block, lanes), BF16 if u else F32) for u in range(ratio)
        ],
        compiler_params=params(),
        name="add_core_near",
    )(mine, theirs, *after)


def add_near(mine, theirs, groups, after=()):
    total, block, lanes = mine.shape
    count = total // groups

    def body(*refs):
        ins, outs = refs[:1 + len(theirs)], refs[1 + len(theirs) + len(after):]
        for n in range(count):
            here = slice(n * groups, (n + 1) * groups)
            acc = ins[0][here]
            for ref in ins[1:]:
                acc = acc + ref[here].astype(F32)
            outs[n][...] = acc.astype(outs[n].dtype)

    return pl.pallas_call(
        body,
        in_specs=[pl.BlockSpec(memory_space=pltpu.VMEM)] * (1 + len(theirs))
        + [pl.BlockSpec(memory_space=pl.ANY)] * len(after),
        out_shape=[jax.ShapeDtypeStruct((groups, block, lanes), BF16 if n else F32) for n in range(count)],
        compiler_params=params(),
        name="add_near",
    )(mine, *theirs, *after)


def fold(parts):
    def body(*refs):
        acc = refs[0][...].astype(F32)
        for ref in refs[1:-1]:
            acc = acc + ref[...].astype(F32)
        refs[-1][...] = acc

    return pl.pallas_call(
        body,
        out_shape=jax.ShapeDtypeStruct(parts[0].shape, F32),
        compiler_params=params(),
        name="fold",
    )(*parts)


def finish(parts, kinds, width, scale):
    groups, block, lanes = parts[0].shape
    ratio = lanes // width

    def body(*refs):
        out = refs[-1]
        for g in range(groups):
            acc = refs[0][g]
            for ref in refs[1:-1]:
                acc = acc + ref[g].astype(F32)
            acc = acc * scale
            for q in range(ratio):
                moved = pltpu.roll(acc, lanes - q * width, 1) if q else acc
                out[g * ratio + q] = moved[:, :width]

    return pl.pallas_call(
        body,
        out_shape=jax.ShapeDtypeStruct((kinds, block, width), F32),
        compiler_params=params(),
        name="finish",
    )(*parts)


def volume_grad(deltas, weights, shape):
    cells_x, cells_y, cells_z, in_chan = shape
    nx, ny, nz = cells_x // 2, cells_y // 2, cells_z // 2
    ratio, rows, out_chan = deltas.shape
    planes = cells_x * cells_y

    def body(d_ref, w_ref, o_hbm, mark_ref, wide_ref, plane_ref, sem):
        mark_ref[...] = jnp.zeros_like(mark_ref)
        row = lax.broadcasted_iota(jnp.int32, (cells_z, nz), 0)
        col = lax.broadcasted_iota(jnp.int32, (cells_z, nz), 1)
        places = sorted({(k % 2, k % ratio) for k in range(8)})
        for n, (e, q) in enumerate(places):
            put = (row == 2 * col + e).astype(F32).astype(BF16)
            for m in range(nx * ny):
                got = jnp.dot(put, d_ref[q, m * nz:(m + 1) * nz], preferred_element_type=F32)
                wide_ref[n, m * cells_z:(m + 1) * cells_z] = got.astype(BF16)
        moves = []
        for a in range(2):
            for b in range(2):
                acc = None
                for e in range(2):
                    k = 4 * a + 2 * b + e
                    part = lax.dot_general(
                        wide_ref[places.index((e, k % ratio))], w_ref[k], (((1,), (1,)), ((), ())),
                        preferred_element_type=F32,
                    )
                    acc = part if acc is None else acc + part
                out = acc.astype(BF16)
                for m in range(nx * ny):
                    x, y = 2 * (m // ny) + a, 2 * (m % ny) + b
                    at = len(moves)
                    plane_ref[at] = out[m * cells_z:(m + 1) * cells_z]
                    move = pltpu.make_async_copy(plane_ref.at[at], o_hbm.at[x, y], sem.at[at])
                    move.start()
                    moves.append(move)
        for move in moves:
            move.wait()

    return pl.pallas_call(
        body,
        in_specs=[pl.BlockSpec(memory_space=pltpu.VMEM)] * 2,
        out_specs=[pl.BlockSpec(memory_space=pl.ANY), pl.BlockSpec(memory_space=pltpu.VMEM)],
        out_shape=[jax.ShapeDtypeStruct(shape, BF16), jax.ShapeDtypeStruct((8, LANES), F32)],
        scratch_shapes=[
            pltpu.VMEM((max(2, ratio), 4 * rows // 2, out_chan), BF16),
            pltpu.VMEM((planes, cells_z, in_chan), BF16),
            pltpu.SemaphoreType.DMA((planes,)),
        ],
        compiler_params=params(),
        cost_estimate=cost(32 * rows * in_chan * out_chan, 2 * rows * 8 * in_chan),
        name="volume_grad",
    )(deltas, weights)


def shards(spaces, chans, volume, weight, cotangent):
    kinds, block, width = weight.shape
    ratio = max(1, LANES // width)
    out_rows = volume.shape[0] * volume.shape[1] * volume.shape[2] // 8

    def pairs(count, step):
        return [(d, other(d, step)) for d in range(count)]

    packed = pack_weight(weight, ratio)
    line = [packed[0]] + [fetch(packed[i % ratio], "chan", pairs(chans, i)) for i in range(1, chans)]
    lane_tiles = chans // ratio
    own = [merge_tile(line[t * ratio:(t + 1) * ratio], width) for t in range(lane_tiles)]
    tiles = pack_cot(cotangent.transpose(0, 1, 3, 2), chans, own[:1])
    cots = [tiles[0]] + [fetch(tiles[i], "chan", pairs(chans, i)) for i in range(1, chans)]
    upstream = turn_cot(cots)
    patches, turned = patch_rows(volume, own[1:])
    lines = []
    for j in range(0, spaces, 2):
        lines.append([fetch(tile, "space", pairs(spaces, j)) for tile in own] if j else own)
        lines.append([fetch(gate(tile, (patches,)) if not j and not t else gate(tile, (patches,)) if not j else gate(tile, (upstream,)) if not t else gate(tile, (upstream,)), "space", pairs(spaces, 1)) for t, tile in enumerate(lines[-1])])
    own_part = None
    if 2 * block % LANES == 0 and spaces > 2:
        own_part = forward_own(patches, lines[:2], spaces, width, ratio)
    deltas, weights = forward(patches, own_part, lines, upstream, width, ratio)
    steps = list(range(0, spaces, 2))
    lanes = ratio * width
    away = weight_part(turned, deltas, [s + 1 for s in steps], spaces, lanes, BF16)
    crossed = [fetch(tile, "space", pairs(spaces, 1)) for tile in away]
    near = weight_part(turned, deltas, steps, spaces, lanes, F32)
    grad_volume, mark = volume_grad(deltas, weights, volume.shape)
    far, outs = [], []
    for t in reversed(range(1, lane_tiles)):
        sums = add_core(near[t], crossed[t])
        far = list(sums[1:]) + far
        came = [fetch(sums[n], "space", pairs(spaces, steps[n])) for n in range(1, len(steps))]
        outs += [(t * ratio + u, part) for u, part in enumerate(add_and_pack(sums[0], came, width, (mark,)))]
    parts = add_core_near(near[0], crossed[0], width, far[:1] + [mark])
    got = [fetch(parts[u], "chan", pairs(chans, u)) for u in range(1, ratio)]
    sums = add_near(parts[0], got, kinds // ratio, [part for _, part in outs[-1:]])
    got = [sums[0]] + [fetch(sums[n], "space", pairs(spaces, steps[n])) for n in range(1, len(steps))]
    spread_out = [fetch(part, "chan", pairs(chans, i)) for i, part in outs]
    got += [fold(spread_out)] if spread_out else []
    grad_weight = finish(got, kinds, width, 1.0 / out_rows)
    return (grad_volume, grad_weight)


def solution(mesh):
    return jax.shard_map(
        functools.partial(shards, mesh.shape["space"], mesh.shape["chan"]),
        mesh=mesh,
        in_specs=(
            P(("groups", "space"), "chan", None, None),
            P(None, "space", "chan"),
            P(("groups", "space"), None, None, "chan"),
        ),
        out_specs=(P(("groups", "space"), "chan", None, None), P("groups", "space", "chan")),
        check_vma=False,
    )
```
